32 devices in a mesh: reg: 4 (over x, core), dam: 8 (over z, y).
Axes of the slice: x: 2, y: 2, z: 4, core: 2. Of those that a mesh axis runs over, the one named last changes fastest.
Arguments:
- history: bfloat16 [4096, 384], P(('reg', 'dam')), may hold values from -6 to 6
- routes: int32 [4096, 2], P(('reg', 'dam')), may hold values from 0 to 31, all different within a row; in each aligned block of 128 rows (0 to 127, 128 to 255, ...) at most 16 rows name the same one
- dam_field: bfloat16 [16384, 384], P(('reg', 'dam')), may hold values from -6 to 6
- conn_free: int32 [2048, 64], P(('reg', 'dam')), may hold values from 0 to 511
- conn_dam: int32 [2048, 64], P(('reg', 'dam')), may hold values from 0 to 511
- stiff_ref: bfloat16 [192, 192], replicated, may hold values from -0.4375 to 0.4375
- stiff_coef: float32 [2048], P(('reg', 'dam')), may hold values from 0.25 to 1
- mass_coef: float32 [2048], P(('reg', 'dam')), may hold values from 0.02 to 0.1
- reg_step: float32 [4096], P(('reg', 'dam')), may hold values from 0.05 to 0.2
- dam_step: float32 [16384], P(('reg', 'dam')), may hold values from 0.05 to 0.2
Outputs:
- history_out: bfloat16 [4096, 384], P(('reg', 'dam'))
- returned_force: float32 [4096, 384], P(('reg', 'dam'))
- dam_out: bfloat16 [16384, 384], P(('reg', 'dam'))
The draws below stay inside these ranges and needn't reach their ends.
Inputs may be any that keep to these rules, and one draw needn't show every extreme that they name: `routes`: in the rows of one device no device number appears more than 16 times; some number appears exactly 16 times in some devices' rows.
All inputs are finite; a program needn't handle non-finite values.
Results may differ from the reference program's by a relative error of at most 0.0047.
Values may be sent and summed in bfloat16 or wider, within the bound.
No kernel may reach another device: no remote copies, remote signals or barrier semaphores. Data moves between devices by JAX's collectives and lax.ppermute only.
A program may use at most 64 MiB of HBM per device.

```python
import math
import jax
import jax.numpy as jnp
import numpy as np
from jax import lax

SAMPLES = 128
NODES = 64
ROUNDS = 2
RB_DEV = 128
ELEM_DEV = 64
DNODE_DEV = 512
CAP = 16
RB_TOTAL = 4096
ELEM_TOTAL = 2048
DNODE_TOTAL = 16384
DEVICES = 32


def with_ends(values, own_key, smallest, top_value):
    dims = values.shape
    index_at = [jax.random.randint(jax.random.fold_in(own_key, axis), (), 0, dims[axis]) for axis in range(len(dims))]
    values = values.at[tuple(index_at)].set(smallest)
    longest = dims.index(max(dims))
    index_at[longest] = (index_at[longest] + 1) % dims[longest]
    return values.at[tuple(index_at)].set(top_value)


def steps_of(own_key, extent, split, least, top_value):
    level, own = 1.0, jax.random.fold_in(own_key, 6)
    for axis_at, parts in split:
        steps = jnp.exp(jax.random.uniform(jax.random.fold_in(own, axis_at), (parts,), jnp.float32, least / len(split), top_value / len(split)))
        level = level * jnp.repeat(steps, extent[axis_at] // parts).reshape([-1 if axis == axis_at else 1 for axis in range(len(extent))])
    return level


def deal_out(rng, own, number, rows, number_of, top, reach, skew):
    ranking = jax.random.permutation(rng, number_of)
    packed, common = load_shares(number_of, rows * top, reach, skew, True), load_shares(number_of, rows * top, reach, skew, False)
    places = jnp.arange(number_of)

    def named(tallies, turn):
        used = int((tallies > 0).sum())
        fixed = max(1, used // 4)
        passed = fixed + (places - fixed + turn * (used - fixed)) % max(1, number_of - fixed)
        return jnp.zeros((number_of,), jnp.int32).at[ranking[jnp.where(places < fixed, places, passed)]].set(jnp.asarray(tallies, jnp.int32))

    tallies = jnp.where(number % 4 == 0, named(packed, number // 4), named(common, number - number // 4 - 1))
    mixed = jax.random.permutation(jax.random.fold_in(own, 3), number_of)
    donor, receiver = mixed[0:number_of // 2 * 2:2], mixed[1:number_of // 2 * 2:2]
    margin = jnp.minimum(tallies[donor] - 1, reach - tallies[receiver]) // 2
    margin = jnp.where((donor == ranking[0]) | (receiver == ranking[0]) | (tallies[receiver] == 0), 0, jnp.maximum(margin, 0))
    passed = jax.random.randint(jax.random.fold_in(own, 4), (number_of // 2,), 0, 1 << 20) % (margin + 1)
    tallies = tallies.at[donor].add(-passed).at[receiver].add(passed)
    members = jnp.searchsorted(jnp.cumsum(tallies), jnp.arange(rows * top), side="right").astype(jnp.int32)
    grid = members.reshape(top, rows).T
    grid = grid[jax.random.permutation(jax.random.fold_in(own, 1), rows)]
    turn = jax.random.randint(jax.random.fold_in(own, 2), (rows, 1), 0, top)
    return jnp.take_along_axis(grid, (jnp.arange(top)[None, :] + turn) % top, axis=1)


def load_shares(amount, total, bound, lean, full):
    weights = [(1 << 20) // math.isqrt(standing ** lean) + 1 for standing in range(1, amount + 1)]
    largest = bound if full else min(bound, max(-(-total // amount), total * weights[0] // sum(weights)))
    least = 1 if total - largest >= amount - 1 else 0
    given, rest = [largest] + [least] * (amount - 1), total - largest - least * (amount - 1)
    while rest > 0:
        movable = [i for i in range(1, amount) if given[i] < largest] or [i for i in range(1, amount) if given[i] < bound]
        mass, remaining = sum([weights[i] for i in movable]), rest
        for i in movable:
            extra = min(bound - given[i], max(1, remaining * weights[i] // mass), rest)
            given[i] = given[i] + extra
            rest = rest - extra
    return np.array(given)


def centred(stream_key, extent, spread, reach, cuts=(), held_as=jnp.bfloat16):
    level = steps_of(stream_key, extent, cuts, -0.22, 0.18) if cuts else 1.0
    values = jax.random.normal(stream_key, extent, jnp.float32) * spread * level
    return jnp.minimum(jnp.maximum(values, -reach), reach).astype(held_as)


def setup_inputs(seed: int = 0) -> dict:
    streams_of = jax.random.split(jax.random.key(seed), 11)
    history = centred(streams_of[0], (RB_TOTAL, 3 * SAMPLES), 1.0, 6.0, ((0, 32),))
    routes_keys = jax.random.split(jax.random.fold_in(streams_of[1], 1), RB_TOTAL // RB_DEV)
    routes_turns = jax.random.permutation(jax.random.fold_in(streams_of[1], 3), RB_TOTAL // RB_DEV)
    routes = jax.vmap(lambda own, number: deal_out(jax.random.fold_in(streams_of[1], 2), own, number, RB_DEV, DEVICES, 2, CAP, 2))(routes_keys, routes_turns).reshape((RB_TOTAL, 2))
    dam_field = centred(streams_of[2], (DNODE_TOTAL, 3 * SAMPLES), 1.0, 6.0, ((0, 32),))
    conn_free = with_ends(jax.random.randint(streams_of[3], (ELEM_TOTAL, NODES), 0, DEVICES * CAP), jax.random.fold_in(streams_of[3], 1), 0, (DEVICES * CAP) - 1).astype(jnp.int32)
    conn_dam = with_ends(jax.random.randint(streams_of[4], (ELEM_TOTAL, NODES), 0, DNODE_DEV), jax.random.fold_in(streams_of[4], 1), 0, DNODE_DEV - 1).astype(jnp.int32)
    stiff_ref = centred(streams_of[5], (3 * NODES, 3 * NODES), (3 * NODES) ** -0.5, 0.4375)
    stiff_coef = jnp.clip(jnp.exp(math.log(1.0) - 1.3862944 * jax.random.uniform(streams_of[6], (ELEM_TOTAL,), jnp.float32) ** steps_of(streams_of[6], (ELEM_TOTAL,), ((0, 32),), -0.2, 0.2)), 0.25, 1.0)
    mass_coef = jnp.clip(jnp.exp(math.log(0.1) - 1.609438 * jax.random.uniform(streams_of[7], (ELEM_TOTAL,), jnp.float32) ** steps_of(streams_of[7], (ELEM_TOTAL,), ((0, 32),), -0.2, 0.2)), 0.02, 0.1)
    reg_step = jnp.clip(jnp.exp(math.log(0.2) - 1.3862944 * jax.random.uniform(streams_of[8], (RB_TOTAL,), jnp.float32) ** steps_of(streams_of[8], (RB_TOTAL,), ((0, 32),), -0.2, 0.2)), 0.05, 0.2)
    dam_step = jnp.clip(jnp.exp(math.log(0.2) - 1.3862944 * jax.random.uniform(streams_of[9], (DNODE_TOTAL,), jnp.float32) ** steps_of(streams_of[9], (DNODE_TOTAL,), ((0, 32),), -0.2, 0.2)), 0.05, 0.2)
    return {"history": history, "routes": routes, "dam_field": dam_field, "conn_free": conn_free, "conn_dam": conn_dam, "stiff_ref": stiff_ref, "stiff_coef": stiff_coef, "mass_coef": mass_coef, "reg_step": reg_step, "dam_step": dam_step}


def element_force(u_free, u_dam, stiff_ref, stiff_part, mass_part):
    count, nodes, row_width = u_free.shape
    samples = row_width // 3
    free_mat = u_free.astype(jnp.float32).reshape(count, nodes * 3, samples)
    dam_mat = u_dam.astype(jnp.float32).reshape(count, nodes * 3, samples)
    stiff_full = stiff_ref.astype(jnp.float32)
    stiff_sum = jnp.einsum("ij,ejt->eit", stiff_full, free_mat) + jnp.einsum("ij,ejt->eit", stiff_full, dam_mat)
    total = free_mat + dam_mat
    padded = jnp.pad(total, ((0, 0), (0, 0), (1, 1)))
    accel = padded[:, :, 2:] - 2.0 * total + padded[:, :, :-2]
    force = stiff_part[:, None, None] * stiff_sum + mass_part[:, None, None] * accel
    return force.reshape(count, nodes, row_width)


def inverse_table(routes):
    entries = routes.reshape(DEVICES, 2 * RB_DEV).astype(jnp.int32)
    numbers = jnp.arange(DEVICES, dtype=jnp.int32)
    onehot = (entries[:, :, None] == numbers[None, None, :]).astype(jnp.int32)
    before = jnp.cumsum(onehot, axis=1) - onehot
    slot = jnp.sum(before * onehot, axis=2).astype(jnp.int32)
    source = jnp.arange(DEVICES, dtype=jnp.int32)[:, None]
    column = (source * CAP + slot).astype(jnp.int32)
    row_id = (jnp.arange(2 * RB_TOTAL, dtype=jnp.int32) // 2).reshape(DEVICES, 2 * RB_DEV)
    table = jnp.full((DEVICES, DEVICES * CAP), -1, dtype=jnp.int32)
    return table.at[entries, column].set(row_id)


def reference(history, routes, dam_field, conn_free, conn_dam, stiff_ref, stiff_coef, mass_coef, reg_step, dam_step):
    row_width = history.shape[1]
    inverse = inverse_table(routes)
    free_dev = conn_free.reshape(DEVICES, ELEM_DEV, NODES)
    dam_refs_dev = conn_dam.reshape(DEVICES, ELEM_DEV, NODES)
    stiff_dev = stiff_coef.reshape(DEVICES, ELEM_DEV)
    mass_dev = mass_coef.reshape(DEVICES, ELEM_DEV)
    damstep_dev = dam_step.reshape(DEVICES, DNODE_DEV)
    pulled = jnp.zeros((RB_TOTAL, row_width), jnp.float32)
    for round_index in range(ROUNDS):
        dam_dev = dam_field.reshape(DEVICES, DNODE_DEV, row_width)
        current = history

        def per_device(carry, pieces):
            table, free_refs, dam_refs, stiff_part, mass_part, dam_local, step_local = pieces
            targets = table[free_refs]
            live = targets >= 0
            safe = jnp.maximum(targets, 0)
            u_free = jnp.where(live[:, :, None], current[safe], jnp.zeros((), current.dtype))
            u_dam = dam_local[dam_refs]
            force = element_force(u_free, u_dam, stiff_ref, stiff_part, mass_part)
            kept = jnp.where(live[:, :, None], force, jnp.zeros((), jnp.float32))
            carry = carry.at[safe.reshape(-1)].add(kept.reshape(-1, row_width))
            dam_sum = jnp.zeros((DNODE_DEV, row_width), jnp.float32).at[dam_refs.reshape(-1)].add(force.reshape(-1, row_width))
            dam_next = (dam_local.astype(jnp.float32) - step_local[:, None] * dam_sum).astype(jnp.bfloat16)
            return carry, dam_next

        start = jnp.zeros((RB_TOTAL, row_width), jnp.float32)
        pulled, dam_stack = lax.scan(per_device, start, (inverse, free_dev, dam_refs_dev, stiff_dev, mass_dev, dam_dev, damstep_dev))
        history = (history.astype(jnp.float32) - reg_step[:, None] * pulled).astype(jnp.bfloat16)
        dam_field = dam_stack.reshape(DNODE_TOTAL, row_width)
    return (history, pulled, dam_field)
```

```python
import functools

import jax
import jax.numpy as jnp
from jax import lax
from jax.experimental import pallas as pl
from jax.experimental.pallas import tpu as pltpu
from jax.sharding import PartitionSpec as P

ROUNDS = 2
GROUP = 8
VMEM_BYTES = 48 * 1024 * 1024
BF16 = jnp.bfloat16
F32 = jnp.float32


def params():
    return pltpu.CompilerParams(vmem_limit_bytes=VMEM_BYTES)


def mask_to_bf16(mask):
    return jnp.where(mask, 1.0, 0.0).astype(BF16)


def select_by_row(columns, width):
    nodes, count = columns.shape
    lanes = lax.broadcasted_iota(jnp.int32, (nodes, width), 1)
    parts = [mask_to_bf16(columns[:, g : g + 1] == lanes) for g in range(count)]
    return jnp.concatenate(parts, axis=0)


def select_by_column(row, width):
    numbers = lax.broadcasted_iota(jnp.int32, (width, row.shape[1]), 0)
    return mask_to_bf16(row == numbers)


def as_column(row):
    size = row.shape[1]
    down = lax.broadcasted_iota(jnp.int32, (size, size), 0)
    across = lax.broadcasted_iota(jnp.int32, (size, size), 1)
    return jnp.sum(jnp.where(down == across, row, 0), axis=1, keepdims=True)


def places_by_row(routes, capacity):
    rows = routes.shape[1]
    row0, row1 = routes[0:1, :], routes[1:2, :]
    col0, col1 = as_column(row0), as_column(row1)
    down = lax.broadcasted_iota(jnp.int32, (rows, rows), 0)
    across = lax.broadcasted_iota(jnp.int32, (rows, rows), 1)
    out = []
    for own in (row0, row1):
        same = jnp.where(col0 == own, 1, 0) + jnp.where(col1 == own, 1, 0)
        slot = jnp.sum(jnp.where(down < across, same, 0), axis=0, keepdims=True)
        out.append(own * capacity + slot)
    return out


def pack_rows(places, history, slots):
    numbers = lax.broadcasted_iota(jnp.int32, (slots, history.shape[0]), 0)
    select = mask_to_bf16((places[0] == numbers) | (places[1] == numbers))
    return jnp.dot(select, history, preferred_element_type=F32).astype(BF16)


def pull_rows(places, returned):
    rows, slots = places[0].shape[1], returned.shape[0]
    lanes = lax.broadcasted_iota(jnp.int32, (rows, slots), 1)
    select = mask_to_bf16((as_column(places[0]) == lanes) | (as_column(places[1]) == lanes))
    return jnp.dot(select, returned, preferred_element_type=F32)


def pack_kernel(capacity, routes_ref, history_ref, out_ref):
    places = places_by_row(routes_ref[...], capacity)
    out_ref[...] = pack_rows(places, history_ref[...], out_ref.shape[0])


def turn_kernel(capacity, routes_ref, returned_ref, history_ref, step_ref, next_ref, out_ref):
    places = places_by_row(routes_ref[...], capacity)
    pulled = pull_rows(places, returned_ref[...])
    step = as_column_f32(step_ref[...])
    following = (history_ref[...].astype(F32) - step * pulled).astype(BF16)
    next_ref[...] = following
    out_ref[...] = pack_rows(places, following, out_ref.shape[0])


def last_kernel(capacity, routes_ref, returned_ref, history_ref, step_ref, next_ref, pulled_ref):
    places = places_by_row(routes_ref[...], capacity)
    pulled = pull_rows(places, returned_ref[...])
    step = as_column_f32(step_ref[...])
    next_ref[...] = (history_ref[...].astype(F32) - step * pulled).astype(BF16)
    pulled_ref[...] = pulled


def as_column_f32(row):
    size = row.shape[1]
    down = lax.broadcasted_iota(jnp.int32, (size, size), 0)
    across = lax.broadcasted_iota(jnp.int32, (size, size), 1)
    return jnp.sum(jnp.where(down == across, row, 0.0), axis=1, keepdims=True)


def gather_kernel(columns_ref, table_ref, out_ref):
    select = select_by_row(columns_ref[0], table_ref.shape[0])
    out_ref[...] = jnp.dot(select, table_ref[...], preferred_element_type=F32).astype(BF16)


def force_kernel(
    columns_ref,
    row_ref,
    received_ref,
    other_ref,
    stiff_ref,
    stiff_coef_ref,
    mass_coef_ref,
    force_ref,
    back_ref,
    total_ref,
):
    step = pl.program_id(0)
    slots, width = received_ref.shape
    nodes = columns_ref.shape[1]
    group = columns_ref.shape[2]
    samples = width // 3
    select = select_by_row(columns_ref[0], slots)
    w = jnp.dot(select, received_ref[...], preferred_element_type=F32)
    w = w + other_ref[...].astype(F32)
    wb = w.astype(BF16)
    stiff = stiff_ref[...]
    lane = lax.broadcasted_iota(jnp.int32, (nodes, samples), 1)
    blocks = []
    for pair in range(0, group, 2):
        sides = [
            jnp.concatenate(
                [
                    wb[e * nodes : (e + 1) * nodes, c * samples : (c + 1) * samples]
                    for c in range(3)
                ],
                axis=0,
            )
            for e in (pair, pair + 1)
        ]
        product = jnp.dot(stiff, jnp.concatenate(sides, axis=1), preferred_element_type=F32)
        for side, e in enumerate((pair, pair + 1)):
            k = stiff_coef_ref[step * group + e]
            m = mass_coef_ref[step * group + e]
            row = []
            for c in range(3):
                part = w[e * nodes : (e + 1) * nodes, c * samples : (c + 1) * samples]
                before = jnp.where(lane == 0, 0.0, pltpu.roll(part, 1, 1))
                after = jnp.where(lane == samples - 1, 0.0, pltpu.roll(part, samples - 1, 1))
                accel = after - 2.0 * part + before
                own = product[c * nodes : (c + 1) * nodes, side * samples : (side + 1) * samples]
                row.append((k * own + m * accel).astype(BF16))
            blocks.append(jnp.concatenate(row, axis=1))
    force = jnp.concatenate(blocks, axis=0)
    force_ref[...] = force
    part = jnp.dot(
        select_by_column(row_ref[0], slots), force, preferred_element_type=F32
    )

    @pl.when(step == 0)
    def _():
        total_ref[...] = part

    @pl.when(step > 0)
    def _():
        total_ref[...] += part

    @pl.when(step == pl.num_programs(0) - 1)
    def _():
        back_ref[...] = total_ref[...].astype(BF16)


def dam_kernel(row_ref, force_ref, dam_ref, step_ref, next_ref, total_ref):
    step = pl.program_id(0)
    part = jnp.dot(
        select_by_column(row_ref[0], dam_ref.shape[0]), force_ref[...], preferred_element_type=F32
    )

    @pl.when(step == 0)
    def _():
        total_ref[...] = part

    @pl.when(step > 0)
    def _():
        total_ref[...] += part

    @pl.when(step == pl.num_programs(0) - 1)
    def _():
        factor = as_column_f32(step_ref[...])
        next_ref[...] = (dam_ref[...].astype(F32) - factor * total_ref[...]).astype(BF16)


def whole(shape):
    return pl.BlockSpec(shape, lambda i: (0,) * len(shape))


def exchange(rows, devices, capacity):
    width = rows.shape[1]
    shaped = rows.reshape(devices, capacity, width)
    arrived = lax.all_to_all(shaped, ("reg", "dam"), split_axis=0, concat_axis=0, tiled=True)
    return arrived.reshape(devices * capacity, width)


def shards(
    history,
    routes,
    dam_field,
    conn_free,
    conn_dam,
    stiff_ref,
    stiff_coef,
    mass_coef,
    reg_step,
    dam_step,
):
    devices = lax.axis_size(("reg", "dam"))
    row_count, width = history.shape
    capacity = 4 * row_count // devices
    slots = devices * capacity
    dam_count = dam_field.shape[0]
    elements, nodes = conn_free.shape
    samples = width // 3
    steps = elements // GROUP
    pairs = GROUP * nodes

    routes_t = routes.T
    reg_row = reg_step.reshape(1, row_count)
    dam_row = dam_step.reshape(1, dam_count)
    free_cols = conn_free.reshape(steps, GROUP, nodes).transpose(0, 2, 1)
    dam_cols = conn_dam.reshape(steps, GROUP, nodes).transpose(0, 2, 1)
    free_rows = conn_free.reshape(steps, 1, pairs)
    dam_rows = conn_dam.reshape(steps, 1, pairs)
    stiff = stiff_ref.reshape(nodes, 3, nodes, 3).transpose(1, 0, 3, 2).reshape(3 * nodes, 3 * nodes)

    cols_spec = pl.BlockSpec((1, nodes, GROUP), lambda i: (i, 0, 0))
    rows_spec = pl.BlockSpec((1, 1, pairs), lambda i: (i, 0, 0))
    pairs_spec = pl.BlockSpec((pairs, width), lambda i: (i, 0))
    scalars = pl.BlockSpec(memory_space=pltpu.SMEM)
    shape = jax.ShapeDtypeStruct
    matmul = 2 * elements * nodes * slots * width

    def cost(flops, moved):
        return pl.CostEstimate(flops=flops, bytes_accessed=moved, transcendentals=0)

    gather = pl.pallas_call(
        gather_kernel,
        name="gather_dam",
        grid=(steps,),
        in_specs=[cols_spec, whole((dam_count, width))],
        out_specs=pairs_spec,
        out_shape=shape((elements * nodes, width), BF16),
        compiler_params=params(),
        cost_estimate=cost(matmul, 2 * elements * nodes * width),
    )
    forces = pl.pallas_call(
        force_kernel,
        name="forces",
        grid=(steps,),
        in_specs=[
            cols_spec,
            rows_spec,
            whole((slots, width)),
            pairs_spec,
            whole(stiff.shape),
            scalars,
            scalars,
        ],
        out_specs=[pairs_spec, whole((slots, width))],
        out_shape=[shape((elements * nodes, width), BF16), shape((slots, width), BF16)],
        scratch_shapes=[pltpu.VMEM((slots, width), F32)],
        compiler_params=params(),
        cost_estimate=cost(3 * matmul, 4 * elements * nodes * width),
    )
    dam_update = pl.pallas_call(
        dam_kernel,
        name="dam_update",
        grid=(steps,),
        in_specs=[rows_spec, pairs_spec, whole((dam_count, width)), whole((1, dam_count))],
        out_specs=whole((dam_count, width)),
        out_shape=shape((dam_count, width), BF16),
        scratch_shapes=[pltpu.VMEM((dam_count, width), F32)],
        compiler_params=params(),
        cost_estimate=cost(matmul, 2 * elements * nodes * width),
    )
    pack = pl.pallas_call(
        functools.partial(pack_kernel, capacity),
        name="pack",
        out_shape=shape((slots, width), BF16),
        compiler_params=params(),
    )
    turn = pl.pallas_call(
        functools.partial(turn_kernel, capacity),
        name="turn",
        out_shape=[shape((row_count, width), BF16), shape((slots, width), BF16)],
        compiler_params=params(),
    )
    last = pl.pallas_call(
        functools.partial(last_kernel, capacity),
        name="last",
        out_shape=[shape((row_count, width), BF16), shape((row_count, width), F32)],
        compiler_params=params(),
    )

    outgoing = pack(routes_t, history)
    for round_index in range(ROUNDS):
        received = exchange(outgoing, devices, capacity)
        u_dam = gather(dam_cols, dam_field)
        force, back = forces(
            free_cols, free_rows, received, u_dam, stiff, stiff_coef, mass_coef
        )
        returned = exchange(back, devices, capacity)
        dam_field = dam_update(dam_rows, force, dam_field, dam_row)
        if round_index < ROUNDS - 1:
            history, outgoing = turn(routes_t, returned, history, reg_row)
        else:
            history, pulled = last(routes_t, returned, history, reg_row)
    return (history, pulled, dam_field)


def solution(mesh):
    rows = P(("reg", "dam"), None)
    flat = P(("reg", "dam"))
    in_specs = (rows, rows, rows, rows, rows, P(), flat, flat, flat, flat)
    return jax.shard_map(
        shards, mesh=mesh, in_specs=in_specs, out_specs=(rows, rows, rows), check_vma=False
    )
```

```python
import functools

import jax
import jax.numpy as jnp
from jax import lax
from jax.experimental import pallas as pl
from jax.experimental.pallas import tpu as pltpu
from jax.sharding import PartitionSpec as P

ROUNDS = 2
GROUP = 8
VMEM_BYTES = 20 * 1024 * 1024
BF16 = jnp.bfloat16
F32 = jnp.float32


def mask_to_bf16(mask):
    return jnp.where(mask, 1.0, 0.0).astype(BF16)


def dot(left, right):
    return jnp.dot(left, right, preferred_element_type=F32)


def dot_first(left, right):
    return lax.dot_general(left, right, (((0,), (0,)), ((), ())), preferred_element_type=F32)


def as_column(row):
    size = row.shape[1]
    down = lax.broadcasted_iota(jnp.int32, (size, size), 0)
    across = lax.broadcasted_iota(jnp.int32, (size, size), 1)
    return jnp.sum(jnp.where(down == across, row, jnp.zeros_like(row)), axis=1, keepdims=True)


def pack_kernel(capacity, routes_ref, history_ref, out_ref, place_ref):
    slots, rows = place_ref.shape
    row0, row1 = routes_ref[0:1, :], routes_ref[1:2, :]
    col0, col1 = as_column(row0), as_column(row1)
    down = lax.broadcasted_iota(jnp.int32, (rows, rows), 0)
    across = lax.broadcasted_iota(jnp.int32, (rows, rows), 1)
    numbers = lax.broadcasted_iota(jnp.int32, (slots, rows), 0)
    hits = []
    for own in (row0, row1):
        same = jnp.where(col0 == own, 1, 0) + jnp.where(col1 == own, 1, 0)
        slot = jnp.sum(jnp.where(down < across, same, 0), axis=0, keepdims=True)
        hits.append(own * capacity + slot == numbers)
    place = mask_to_bf16(hits[0] | hits[1])
    place_ref[...] = place
    out_ref[...] = dot(place, history_ref[...]).astype(BF16)


def turn_kernel(place_ref, returned_ref, history_ref, step_ref, next_ref, out_ref):
    place = place_ref[...]
    pulled = dot_first(place, returned_ref[...])
    following = (history_ref[...].astype(F32) - step_ref[:, 0:1] * pulled).astype(BF16)
    next_ref[...] = following
    out_ref[...] = dot(place, following).astype(BF16)


def last_kernel(place_ref, returned_ref, history_ref, step_ref, next_ref, pulled_ref):
    pulled = dot_first(place_ref[...], returned_ref[...])
    next_ref[...] = (history_ref[...].astype(F32) - step_ref[:, 0:1] * pulled).astype(BF16)
    pulled_ref[...] = pulled


def select_rows(conn_ref, select_ref):
    elements, nodes = conn_ref.shape
    columns = conn_ref[...].T
    lanes = lax.broadcasted_iota(jnp.int32, (nodes, select_ref.shape[1]), 1)
    for e in range(elements):
        select_ref[e * nodes : (e + 1) * nodes, :] = mask_to_bf16(columns[:, e : e + 1] == lanes)


def prepare_kernel(
    free_ref,
    dam_ref,
    stiff_ref,
    reg_ref,
    step_ref,
    free_select_ref,
    dam_select_ref,
    order_ref,
    reg_out_ref,
    step_out_ref,
):
    select_rows(free_ref, free_select_ref)
    select_rows(dam_ref, dam_select_ref)
    size = stiff_ref.shape[0]
    nodes = size // 3
    down = lax.broadcasted_iota(jnp.int32, (size, size), 0)
    across = lax.broadcasted_iota(jnp.int32, (size, size), 1)
    part = (down >= nodes).astype(jnp.int32) + (down >= 2 * nodes).astype(jnp.int32)
    order = mask_to_bf16(across == 3 * (down - part * nodes) + part)
    half = dot(order, stiff_ref[...]).astype(BF16)
    order_ref[...] = lax.dot_general(
        half, order, (((1,), (1,)), ((), ())), preferred_element_type=F32
    ).astype(BF16)
    reg_out_ref[...] = jnp.broadcast_to(as_column(reg_ref[...]), reg_out_ref.shape)
    step_out_ref[...] = jnp.broadcast_to(as_column(step_ref[...]), step_out_ref.shape)


def element_forces(u, stiff, stiff_coef_ref, mass_coef_ref, first, count):
    nodes = u.shape[0] // count
    samples = u.shape[1] // 3
    lane = lax.broadcasted_iota(jnp.int32, (nodes, samples), 1)

    def part(e, c):
        return u[e * nodes : (e + 1) * nodes, c * samples : (c + 1) * samples]

    blocks = []
    for pair in range(0, count, 2):
        sides = [jnp.concatenate([part(e, c) for c in range(3)], axis=0) for e in (pair, pair + 1)]
        product = dot(stiff, jnp.concatenate(sides, axis=1))
        for side, e in enumerate((pair, pair + 1)):
            k = stiff_coef_ref[first + e]
            m = mass_coef_ref[first + e]
            row = []
            for c in range(3):
                own = product[c * nodes : (c + 1) * nodes, side * samples : (side + 1) * samples]
                w = part(e, c).astype(F32)
                before = jnp.where(lane == 0, 0.0, pltpu.roll(w, 1, 1))
                after = jnp.where(lane == samples - 1, 0.0, pltpu.roll(w, samples - 1, 1))
                row.append((k * own + m * (after - 2.0 * w + before)).astype(BF16))
            blocks.append(jnp.concatenate(row, axis=1))
    return jnp.concatenate(blocks, axis=0)


def sweep(select_ref, table, stiff, coefs, force_ref, held, add):
    pairs = held[0].shape[0]
    groups = select_ref.shape[0] // pairs
    for turn in range(groups + 2):
        if turn >= 2:
            rows = slice((turn - 2) * pairs, (turn - 1) * pairs)
            add(rows, force_ref[rows, :])
        if 1 <= turn <= groups:
            rows = slice((turn - 1) * pairs, turn * pairs)
            u = held[(turn - 1) % 2][...]
            force_ref[rows, :] = element_forces(u, stiff, *coefs, (turn - 1) * GROUP, GROUP)
        if turn < groups:
            rows = slice(turn * pairs, (turn + 1) * pairs)
            held[turn % 2][...] = dot(select_ref[rows, :], table).astype(BF16)


def dam_part_kernel(
    free_select_ref,
    dam_select_ref,
    dam_ref,
    stiff_ref,
    stiff_coef_ref,
    mass_coef_ref,
    back_ref,
    sum_ref,
    force_ref,
    *held,
):
    back_ref[...] = jnp.zeros_like(back_ref)
    sum_ref[...] = jnp.zeros_like(sum_ref)

    def add(rows, force):
        back_ref[...] += dot_first(force, free_select_ref[rows, :])
        sum_ref[...] += dot_first(force, dam_select_ref[rows, :])

    coefs = (stiff_coef_ref, mass_coef_ref)
    sweep(dam_select_ref, dam_ref[...], stiff_ref[...], coefs, force_ref, held, add)


def free_part_kernel(
    select_ref,
    received_ref,
    stiff_ref,
    stiff_coef_ref,
    mass_coef_ref,
    start_ref,
    force_ref,
    back_ref,
    total_ref,
    *held,
):
    total_ref[...] = start_ref[...]

    def add(rows, force):
        total_ref[...] += dot_first(force, select_ref[rows, :])

    coefs = (stiff_coef_ref, mass_coef_ref)
    sweep(select_ref, received_ref[...], stiff_ref[...], coefs, force_ref, held, add)
    back_ref[...] = total_ref[...].T.astype(BF16)


def dam_update_kernel(select_ref, force_ref, start_ref, dam_ref, step_ref, next_ref):
    total = start_ref[...] + dot_first(force_ref[...], select_ref[...])
    next_ref[...] = (dam_ref[...].astype(F32) - step_ref[:, 0:1] * total.T).astype(BF16)


def exchange(rows, devices, capacity):
    width = rows.shape[1]
    shaped = rows.reshape(devices, capacity, width)
    arrived = lax.all_to_all(shaped, ("reg", "dam"), split_axis=0, concat_axis=0, tiled=True)
    return arrived.reshape(devices * capacity, width)


def kernel(body, name, n_in, out_shape, scalars=(), scratch=(), flops=0, moved=0):
    vmem = pl.BlockSpec(memory_space=pltpu.VMEM)
    smem = pl.BlockSpec(memory_space=pltpu.SMEM)
    return pl.pallas_call(
        body,
        name=name,
        in_specs=[smem if i in scalars else vmem for i in range(n_in)],
        out_specs=[vmem] * len(out_shape),
        out_shape=out_shape,
        scratch_shapes=list(scratch),
        compiler_params=pltpu.CompilerParams(vmem_limit_bytes=VMEM_BYTES),
        cost_estimate=pl.CostEstimate(flops=flops, bytes_accessed=moved, transcendentals=0),
    )


def shards(
    history,
    routes,
    dam_field,
    conn_free,
    conn_dam,
    stiff_ref,
    stiff_coef,
    mass_coef,
    reg_step,
    dam_step,
):
    devices = lax.axis_size(("reg", "dam"))
    row_count, width = history.shape
    capacity = 4 * row_count // devices
    slots = devices * capacity
    dam_count = dam_field.shape[0]
    elements, nodes = conn_free.shape
    all_pairs = elements * nodes
    pairs = GROUP * nodes
    lanes = 128

    shape = jax.ShapeDtypeStruct
    product = 2 * all_pairs * slots * width
    held = [pltpu.VMEM((pairs, width), BF16)] * 2

    pack = kernel(
        functools.partial(pack_kernel, capacity),
        "pack",
        2,
        [shape((slots, width), BF16), shape((slots, row_count), BF16)],
    )
    prepare = kernel(
        prepare_kernel,
        "prepare",
        5,
        [
            shape((all_pairs, slots), BF16),
            shape((all_pairs, dam_count), BF16),
            shape(stiff_ref.shape, BF16),
            shape((row_count, lanes), F32),
            shape((dam_count, lanes), F32),
        ],
        flops=product,
        moved=4 * all_pairs * slots,
    )
    dam_part = kernel(
        dam_part_kernel,
        "dam_part",
        6,
        [shape((width, slots), F32), shape((width, dam_count), F32)],
        scalars=(4, 5),
        scratch=[pltpu.VMEM((all_pairs, width), BF16)] + held,
        flops=4 * product,
        moved=4 * all_pairs * slots,
    )
    free_part = kernel(
        free_part_kernel,
        "free_part",
        6,
        [shape((all_pairs, width), BF16), shape((slots, width), BF16)],
        scalars=(3, 4),
        scratch=[pltpu.VMEM((width, slots), F32)] + held,
        flops=3 * product,
        moved=4 * all_pairs * slots,
    )
    dam_update = kernel(
        dam_update_kernel,
        "dam_update",
        5,
        [shape((dam_count, width), BF16)],
        flops=product,
        moved=4 * all_pairs * slots,
    )
    turn = kernel(
        turn_kernel, "turn", 4, [shape((row_count, width), BF16), shape((slots, width), BF16)]
    )
    last = kernel(
        last_kernel, "last", 4, [shape((row_count, width), BF16), shape((row_count, width), F32)]
    )

    outgoing, place = pack(routes.T, history)
    free_select, dam_select, stiff, reg_column, dam_column = prepare(
        conn_free,
        conn_dam,
        stiff_ref,
        reg_step.reshape(1, row_count),
        dam_step.reshape(1, dam_count),
    )
    for round_index in range(ROUNDS):
        received = exchange(outgoing, devices, capacity)
        back_start, sum_start = dam_part(
            free_select, dam_select, dam_field, stiff, stiff_coef, mass_coef
        )
        received, back_start = lax.optimization_barrier((received, back_start))
        force, back = free_part(free_select, received, stiff, stiff_coef, mass_coef, back_start)
        returned = exchange(back, devices, capacity)
        (dam_field,) = dam_update(dam_select, force, sum_start, dam_field, dam_column)
        returned, dam_field = lax.optimization_barrier((returned, dam_field))
        if round_index < ROUNDS - 1:
            history, outgoing = turn(place, returned, history, reg_column)
        else:
            history, pulled = last(place, returned, history, reg_column)
    return (history, pulled, dam_field)


def solution(mesh):
    rows = P(("reg", "dam"), None)
    flat = P(("reg", "dam"))
    in_specs = (rows, rows, rows, rows, rows, P(), flat, flat, flat, flat)
    return jax.shard_map(
        shards, mesh=mesh, in_specs=in_specs, out_specs=(rows, rows, rows), check_vma=False
    )
```

```python
import functools

import jax
import jax.numpy as jnp
from jax import lax
from jax.experimental import pallas as pl
from jax.experimental.pallas import tpu as pltpu
from jax.sharding import PartitionSpec as P

ROUNDS = 2
GROUP = 8
VMEM_BYTES = 28 * 1024 * 1024
BF16 = jnp.bfloat16
F32 = jnp.float32


def mask_to_bf16(mask):
    return jnp.where(mask, 1.0, 0.0).astype(BF16)


def dot(left, right):
    return jnp.dot(left, right, preferred_element_type=F32)


def dot_first(left, right):
    return lax.dot_general(left, right, (((0,), (0,)), ((), ())), preferred_element_type=F32)


def transfer(pairs, sems):
    copies = [pltpu.make_async_copy(a, b, sems.at[i]) for i, (a, b) in enumerate(pairs)]
    for copy in copies:
        copy.start()
    return copies


def finish(copies):
    for copy in copies:
        copy.wait()


def as_column(row):
    size = row.shape[1]
    down = lax.broadcasted_iota(jnp.int32, (size, size), 0)
    across = lax.broadcasted_iota(jnp.int32, (size, size), 1)
    return jnp.sum(jnp.where(down == across, row, jnp.zeros_like(row)), axis=1, keepdims=True)


def pack_kernel(
    capacity, routes_hbm, history_hbm, out_hbm, place_hbm, routes_ref, history_ref, out_ref, place_ref, sems
):
    inward = transfer([(routes_hbm, routes_ref), (history_hbm, history_ref)], sems)
    slots, rows = place_ref.shape
    finish(inward[:1])
    row0, row1 = routes_ref[0:1, :], routes_ref[1:2, :]
    col0, col1 = as_column(row0), as_column(row1)
    down = lax.broadcasted_iota(jnp.int32, (rows, rows), 0)
    across = lax.broadcasted_iota(jnp.int32, (rows, rows), 1)
    numbers = lax.broadcasted_iota(jnp.int32, (slots, rows), 0)
    hits = []
    for own in (row0, row1):
        same = jnp.where(col0 == own, 1, 0) + jnp.where(col1 == own, 1, 0)
        slot = jnp.sum(jnp.where(down < across, same, 0), axis=0, keepdims=True)
        hits.append(own * capacity + slot == numbers)
    place = mask_to_bf16(hits[0] | hits[1])
    place_ref[...] = place
    finish(inward[1:])
    out_ref[...] = dot(place, history_ref[...]).astype(BF16)
    finish(transfer([(out_ref, out_hbm), (place_ref, place_hbm)], sems))


def turn_kernel(
    place_hbm,
    returned_ref,
    history_hbm,
    step_hbm,
    after_hbm,
    next_hbm,
    out_hbm,
    place_ref,
    history_ref,
    step_ref,
    next_ref,
    out_ref,
    sems,
):
    inward = transfer(
        [(place_hbm, place_ref), (history_hbm, history_ref), (step_hbm, step_ref)], sems
    )
    finish(inward)
    place = place_ref[...]
    pulled = dot_first(place, returned_ref[...])
    step = as_column(step_ref[...])
    following = (history_ref[...].astype(F32) - step * pulled).astype(BF16)
    next_ref[...] = following
    out_ref[...] = dot(place, following).astype(BF16)
    finish(transfer([(next_ref, next_hbm), (out_ref, out_hbm)], sems))


def last_kernel(
    place_hbm,
    returned_ref,
    history_hbm,
    step_hbm,
    after_hbm,
    next_hbm,
    pulled_hbm,
    place_ref,
    history_ref,
    step_ref,
    next_ref,
    pulled_ref,
    sems,
):
    inward = transfer(
        [(place_hbm, place_ref), (history_hbm, history_ref), (step_hbm, step_ref)], sems
    )
    finish(inward)
    pulled = dot_first(place_ref[...], returned_ref[...])
    step = as_column(step_ref[...])
    next_ref[...] = (history_ref[...].astype(F32) - step * pulled).astype(BF16)
    pulled_ref[...] = pulled
    finish(transfer([(next_ref, next_hbm), (pulled_ref, pulled_hbm)], sems))


def by_component(stiff):
    size = stiff.shape[0]
    nodes = size // 3
    down = lax.broadcasted_iota(jnp.int32, (size, size), 0)
    across = lax.broadcasted_iota(jnp.int32, (size, size), 1)
    part = (down >= nodes).astype(jnp.int32) + (down >= 2 * nodes).astype(jnp.int32)
    order = mask_to_bf16(across == 3 * (down - part * nodes) + part)
    half = dot(order, stiff).astype(BF16)
    return lax.dot_general(
        half, order, (((1,), (1,)), ((), ())), preferred_element_type=F32
    ).astype(BF16)


def select_rows(columns, first, width):
    nodes = columns.shape[0]
    lanes = lax.broadcasted_iota(jnp.int32, (nodes, width), 1).astype(jnp.int16)
    parts = []
    for e in range(first, first + GROUP):
        own = jnp.broadcast_to(columns[:, e : e + 1], (nodes, width)).astype(jnp.int16)
        parts.append(jnp.where(own == lanes, jnp.ones((), BF16), jnp.zeros((), BF16)))
    return jnp.concatenate(parts, axis=0)


def element_forces(u, stiff, stiff_coef_ref, mass_coef_ref, first):
    nodes = u.shape[0] // GROUP
    samples = u.shape[1] // 3
    lane = lax.broadcasted_iota(jnp.int32, (nodes, samples), 1).astype(jnp.int16)
    nothing = jnp.zeros((), BF16)

    def part(e, c):
        return u[e * nodes : (e + 1) * nodes, c * samples : (c + 1) * samples]

    blocks = []
    for pair in range(0, GROUP, 2):
        sides = [jnp.concatenate([part(e, c) for c in range(3)], axis=0) for e in (pair, pair + 1)]
        product = dot(stiff, jnp.concatenate(sides, axis=1))
        for side, e in enumerate((pair, pair + 1)):
            k = stiff_coef_ref[first + e]
            m = mass_coef_ref[first + e]
            row = []
            for c in range(3):
                own = product[c * nodes : (c + 1) * nodes, side * samples : (side + 1) * samples]
                w = part(e, c)
                before = jnp.where(lane == 0, nothing, pltpu.roll(w, 1, 1))
                after = jnp.where(lane == samples - 1, nothing, pltpu.roll(w, samples - 1, 1))
                accel = ((before + after) - (w + w)).astype(F32)
                row.append((k * own + m * accel).astype(BF16))
            blocks.append(jnp.concatenate(row, axis=1))
    return jnp.concatenate(blocks, axis=0)


def sweep(select, table, stiff, coefs, force_ref, held, add):
    pairs = held[0].shape[0]
    groups = force_ref.shape[0] // pairs
    for turn in range(groups + 3):
        if turn >= 3:
            add(turn - 3, slice((turn - 3) * pairs, (turn - 2) * pairs))
        if 2 <= turn < groups + 2:
            rows = slice((turn - 2) * pairs, (turn - 1) * pairs)
            force_ref[rows, :] = element_forces(
                held[turn % 2][...], stiff, *coefs, (turn - 2) * GROUP
            )
        if 1 <= turn < groups + 1:
            rows = slice((turn - 1) * pairs, turn * pairs)
            held[(turn - 1) % 2][...] = dot(select.made[rows, :], table).astype(BF16)
        if turn < groups:
            select.make(turn)


class Selection:
    def __init__(self, made, columns):
        self.made = made
        self.columns = columns

    def make(self, group):
        pairs = GROUP * self.columns.shape[0]
        self.made[group * pairs : (group + 1) * pairs, :] = select_rows(
            self.columns, group * GROUP, self.made.shape[1]
        )


def dam_part_kernel(
    free_hbm,
    dam_conn_hbm,
    dam_hbm,
    stiff_hbm,
    stiff_coef_hbm,
    mass_coef_hbm,
    back_hbm,
    sum_hbm,
    order_hbm,
    free_ref,
    dam_conn_ref,
    dam_ref,
    stiff_ref,
    stiff_coef_ref,
    mass_coef_ref,
    back_ref,
    sum_ref,
    free_made,
    dam_made,
    force_ref,
    held0,
    held1,
    sems,
):
    inward = transfer(
        [
            (free_hbm, free_ref),
            (dam_conn_hbm, dam_conn_ref),
            (dam_hbm, dam_ref),
            (stiff_hbm, stiff_ref),
            (stiff_coef_hbm, stiff_coef_ref),
            (mass_coef_hbm, mass_coef_ref),
        ],
        sems,
    )
    back_ref[...] = jnp.zeros_like(back_ref)
    sum_ref[...] = jnp.zeros_like(sum_ref)
    finish(inward)
    stiff_ref[...] = by_component(stiff_ref[...])
    outward = transfer([(stiff_ref, order_hbm)], sems)
    free = Selection(free_made, free_ref[...].T)
    dam = Selection(dam_made, dam_conn_ref[...].T)

    def add(group, rows):
        force = force_ref[rows, :]
        free.make(group)
        sum_ref[...] += dot_first(force, dam_made[rows, :])
        back_ref[...] += dot_first(force, free_made[rows, :])

    coefs = (stiff_coef_ref, mass_coef_ref)
    sweep(dam, dam_ref[...], stiff_ref[...], coefs, force_ref, (held0, held1), add)
    finish(outward)
    finish(transfer([(back_ref, back_hbm), (sum_ref, sum_hbm)], sems))


def free_part_kernel(
    free_hbm,
    received_ref,
    stiff_hbm,
    stiff_coef_hbm,
    mass_coef_hbm,
    start_hbm,
    force_hbm,
    back_hbm,
    free_ref,
    stiff_ref,
    stiff_coef_ref,
    mass_coef_ref,
    start_ref,
    total_ref,
    made,
    force_ref,
    back_ref,
    held0,
    held1,
    sems,
    out_sems,
):
    inward = transfer(
        [
            (free_hbm, free_ref),
            (stiff_hbm, stiff_ref),
            (stiff_coef_hbm, stiff_coef_ref),
            (mass_coef_hbm, mass_coef_ref),
            (start_hbm, start_ref),
        ],
        sems,
    )
    finish(inward[:4])
    outward = []

    def add(group, rows):
        own = force_ref.at[rows, :]
        copy = pltpu.make_async_copy(own, force_hbm.at[rows, :], out_sems.at[group])
        copy.start()
        outward.append(copy)
        part = dot_first(own[...], made[rows, :])
        total_ref[...] = part if group == 0 else total_ref[...] + part

    coefs = (stiff_coef_ref, mass_coef_ref)
    select = Selection(made, free_ref[...].T)
    sweep(select, received_ref[...], stiff_ref[...], coefs, force_ref, (held0, held1), add)
    finish(inward[4:])
    back_ref[...] = (start_ref[...] + total_ref[...]).T.astype(BF16)
    finish(transfer([(back_ref, back_hbm)], sems))
    finish(outward)


def dam_update_kernel(
    dam_conn_hbm,
    force_hbm,
    start_hbm,
    dam_hbm,
    step_hbm,
    next_hbm,
    dam_conn_ref,
    force_ref,
    total_ref,
    dam_ref,
    step_ref,
    next_ref,
    made,
    sems,
    in_sems,
):
    inward = transfer(
        [
            (dam_conn_hbm, dam_conn_ref),
            (start_hbm, total_ref),
            (dam_hbm, dam_ref),
            (step_hbm, step_ref),
        ],
        sems,
    )
    nodes = dam_conn_ref.shape[1]
    pairs = GROUP * nodes
    groups = made.shape[0] // pairs
    chunks = [slice(g * pairs, (g + 1) * pairs) for g in range(groups)]
    forces = transfer([(force_hbm.at[rows, :], force_ref.at[rows, :]) for rows in chunks], in_sems)
    finish(inward)
    select = Selection(made, dam_conn_ref[...].T)
    for turn in range(groups + 1):
        if turn >= 1:
            rows = chunks[turn - 1]
            finish(forces[turn - 1 : turn])
            total_ref[...] += dot_first(force_ref[rows, :], made[rows, :])
        if turn < groups:
            select.make(turn)
    step = as_column(step_ref[...])
    next_ref[...] = (dam_ref[...].astype(F32) - step * total_ref[...].T).astype(BF16)
    finish(transfer([(next_ref, next_hbm)], sems))


def exchange(rows, devices, capacity):
    width = rows.shape[1]
    shaped = rows.reshape(devices, capacity, width)
    arrived = lax.all_to_all(shaped, ("reg", "dam"), split_axis=0, concat_axis=0, tiled=True)
    return arrived.reshape(devices * capacity, width)


def kernel(body, name, n_in, outs, scratch, inside=(), flops=0, moved=0):
    hbm = pl.BlockSpec(memory_space=pltpu.HBM)
    vmem = pl.BlockSpec(memory_space=pltpu.VMEM)
    call = pl.pallas_call(
        body,
        name=name,
        in_specs=[vmem if i in inside else hbm for i in range(n_in)],
        out_specs=[hbm] * len(outs),
        out_shape=[pltpu.HBM(*out) for out in outs],
        scratch_shapes=scratch,
        compiler_params=pltpu.CompilerParams(vmem_limit_bytes=VMEM_BYTES),
        cost_estimate=pl.CostEstimate(flops=flops, bytes_accessed=moved, transcendentals=0),
    )

    def run(*operands):
        return call(
            *[
                x if i in inside else pltpu.with_memory_space_constraint(x, pltpu.HBM)
                for i, x in enumerate(operands)
            ]
        )

    return run


def shards(
    history,
    routes,
    dam_field,
    conn_free,
    conn_dam,
    stiff_ref,
    stiff_coef,
    mass_coef,
    reg_step,
    dam_step,
):
    devices = lax.axis_size(("reg", "dam"))
    row_count, width = history.shape
    capacity = 4 * row_count // devices
    slots = devices * capacity
    dam_count = dam_field.shape[0]
    elements, nodes = conn_free.shape
    all_pairs = elements * nodes
    pairs = GROUP * nodes
    groups = elements // GROUP

    I32 = jnp.int32
    vmem = pltpu.VMEM
    dma = pltpu.SemaphoreType.DMA
    conn = vmem((elements, nodes), I32)
    stiff = vmem(stiff_ref.shape, BF16)
    coefs = [pltpu.SMEM((elements,), F32)] * 2
    held = [vmem((pairs, width), BF16)] * 2
    forces = vmem((all_pairs, width), BF16)
    free_made = vmem((all_pairs, slots), BF16)
    dam_made = vmem((all_pairs, dam_count), BF16)
    place_type = ((slots, row_count), BF16)
    slots_type = ((slots, width), BF16)
    rows_type = ((row_count, width), BF16)
    dam_type = ((dam_count, width), BF16)
    product = 2 * all_pairs * slots * width

    pack = kernel(
        functools.partial(pack_kernel, capacity),
        "pack",
        2,
        [slots_type, place_type],
        [vmem((2, row_count), I32), vmem(*rows_type), vmem(*slots_type), vmem(*place_type), dma((2,))],
    )
    turn_scratch = [vmem(*place_type), vmem(*rows_type), vmem((1, row_count), F32), vmem(*rows_type)]
    turn = kernel(
        turn_kernel,
        "turn",
        5,
        [rows_type, slots_type],
        turn_scratch + [vmem(*slots_type), dma((3,))],
        inside=(1,),
    )
    last = kernel(
        last_kernel,
        "last",
        5,
        [rows_type, ((row_count, width), F32)],
        turn_scratch + [vmem((row_count, width), F32), dma((3,))],
        inside=(1,),
    )
    dam_part = kernel(
        dam_part_kernel,
        "dam_part",
        6,
        [((width, slots), F32), ((width, dam_count), F32), (stiff_ref.shape, BF16)],
        [conn, conn, vmem(*dam_type), stiff, *coefs]
        + [vmem((width, slots), F32), vmem((width, dam_count), F32)]
        + [free_made, dam_made, forces, *held, dma((6,))],
        flops=4 * product,
        moved=4 * all_pairs * width,
    )
    free_part = kernel(
        free_part_kernel,
        "free_part",
        6,
        [((all_pairs, width), BF16), slots_type],
        [conn, stiff, *coefs, vmem((width, slots), F32), vmem((width, slots), F32)]
        + [free_made, forces, vmem(*slots_type), *held, dma((5,)), dma((groups,))],
        inside=(1,),
        flops=3 * product,
        moved=4 * all_pairs * width,
    )
    dam_update = kernel(
        dam_update_kernel,
        "dam_update",
        5,
        [dam_type],
        [conn, forces, vmem((width, dam_count), F32), vmem(*dam_type), vmem((1, dam_count), F32)]
        + [vmem(*dam_type), dam_made, dma((4,)), dma((groups,))],
        flops=product,
        moved=4 * all_pairs * width,
    )

    reg_row = reg_step.reshape(1, row_count)
    dam_row = dam_step.reshape(1, dam_count)
    outgoing, place = pack(routes.T, history)
    for round_index in range(ROUNDS):
        received = exchange(outgoing, devices, capacity)
        back_start, sum_start, ordered = dam_part(
            conn_free, conn_dam, dam_field, stiff_ref, stiff_coef, mass_coef
        )
        force, back = free_part(conn_free, received, ordered, stiff_coef, mass_coef, back_start)
        returned = exchange(back, devices, capacity)
        (dam_field,) = dam_update(conn_dam, force, sum_start, dam_field, dam_row)
        if round_index < ROUNDS - 1:
            history, outgoing = turn(place, returned, history, reg_row, dam_field)
        else:
            history, pulled = last(place, returned, history, reg_row, dam_field)
    return (history, pulled, dam_field)


def solution(mesh):
    rows = P(("reg", "dam"), None)
    flat = P(("reg", "dam"))
    in_specs = (rows, rows, rows, rows, rows, P(), flat, flat, flat, flat)
    return jax.shard_map(
        shards, mesh=mesh, in_specs=in_specs, out_specs=(rows, rows, rows), check_vma=False
    )
```

```python
import functools

import jax
import jax.numpy as jnp
from jax import lax
from jax.experimental import pallas as pl
from jax.experimental.pallas import tpu as pltpu
from jax.sharding import PartitionSpec as P

ROUNDS = 2
GROUP = 8
VMEM_BYTES = 28 * 1024 * 1024
BF16 = jnp.bfloat16
F32 = jnp.float32


def mask_to_bf16(mask):
    return jnp.where(mask, 1.0, 0.0).astype(BF16)


def dot(left, right):
    return jnp.dot(left, right, preferred_element_type=F32)


def dot_first(left, right):
    return lax.dot_general(left, right, (((0,), (0,)), ((), ())), preferred_element_type=F32)


def transfer(pairs, sems):
    copies = [pltpu.make_async_copy(a, b, sems.at[i]) for i, (a, b) in enumerate(pairs)]
    for copy in copies:
        copy.start()
    return copies


def finish(copies):
    for copy in copies:
        copy.wait()


def as_column(row):
    size = row.shape[1]
    down = lax.broadcasted_iota(jnp.int32, (size, size), 0)
    across = lax.broadcasted_iota(jnp.int32, (size, size), 1)
    return jnp.sum(jnp.where(down == across, row, jnp.zeros_like(row)), axis=1, keepdims=True)


def pack_kernel(
    capacity, routes_hbm, history_hbm, out_hbm, place_hbm, routes_ref, history_ref, out_ref, place_ref, sems
):
    inward = transfer([(routes_hbm, routes_ref), (history_hbm, history_ref)], sems)
    slots, rows = place_ref.shape
    finish(inward[:1])
    row0, row1 = routes_ref[0:1, :], routes_ref[1:2, :]
    col0, col1 = as_column(row0), as_column(row1)
    down = lax.broadcasted_iota(jnp.int32, (rows, rows), 0)
    across = lax.broadcasted_iota(jnp.int32, (rows, rows), 1)
    numbers = lax.broadcasted_iota(jnp.int32, (slots, rows), 0)
    hits = []
    for own in (row0, row1):
        same = jnp.where(col0 == own, 1, 0) + jnp.where(col1 == own, 1, 0)
        slot = jnp.sum(jnp.where(down < across, same, 0), axis=0, keepdims=True)
        hits.append(own * capacity + slot == numbers)
    place = mask_to_bf16(hits[0] | hits[1])
    place_ref[...] = place
    finish(inward[1:])
    out_ref[...] = dot(place, history_ref[...]).astype(BF16)
    finish(transfer([(out_ref, out_hbm), (place_ref, place_hbm)], sems))


def turn_kernel(
    place_hbm,
    returned_ref,
    history_hbm,
    step_hbm,
    after_hbm,
    next_hbm,
    out_hbm,
    place_ref,
    history_ref,
    step_ref,
    next_ref,
    out_ref,
    sems,
):
    inward = transfer(
        [(place_hbm, place_ref), (history_hbm, history_ref), (step_hbm, step_ref)], sems
    )
    finish(inward)
    place = place_ref[...]
    pulled = dot_first(place, returned_ref[...])
    step = as_column(step_ref[...])
    following = (history_ref[...].astype(F32) - step * pulled).astype(BF16)
    next_ref[...] = following
    out_ref[...] = dot(place, following).astype(BF16)
    finish(transfer([(next_ref, next_hbm), (out_ref, out_hbm)], sems))


def last_kernel(
    place_hbm,
    returned_ref,
    history_hbm,
    step_hbm,
    after_hbm,
    next_hbm,
    pulled_hbm,
    place_ref,
    history_ref,
    step_ref,
    next_ref,
    pulled_ref,
    sems,
):
    inward = transfer(
        [(place_hbm, place_ref), (history_hbm, history_ref), (step_hbm, step_ref)], sems
    )
    finish(inward)
    pulled = dot_first(place_ref[...], returned_ref[...])
    step = as_column(step_ref[...])
    next_ref[...] = (history_ref[...].astype(F32) - step * pulled).astype(BF16)
    pulled_ref[...] = pulled
    finish(transfer([(next_ref, next_hbm), (pulled_ref, pulled_hbm)], sems))


def by_component(stiff):
    size = stiff.shape[0]
    nodes = size // 3
    down = lax.broadcasted_iota(jnp.int32, (size, size), 0)
    across = lax.broadcasted_iota(jnp.int32, (size, size), 1)
    part = (down >= nodes).astype(jnp.int32) + (down >= 2 * nodes).astype(jnp.int32)
    order = mask_to_bf16(across == 3 * (down - part * nodes) + part)
    half = dot(order, stiff).astype(BF16)
    return lax.dot_general(
        half, order, (((1,), (1,)), ((), ())), preferred_element_type=F32
    ).astype(BF16)


def select_rows(columns, first, width):
    nodes = columns.shape[0]
    lanes = lax.broadcasted_iota(jnp.int32, (nodes, width), 1).astype(jnp.int16)
    parts = []
    for e in range(first, first + GROUP):
        own = jnp.broadcast_to(columns[:, e : e + 1], (nodes, width)).astype(jnp.int16)
        parts.append(jnp.where(own == lanes, jnp.ones((), BF16), jnp.zeros((), BF16)))
    return jnp.concatenate(parts, axis=0)


def element_forces(u, stiff, stiff_coef_ref, mass_coef_ref, first):
    nodes = u.shape[0] // GROUP
    samples = u.shape[1] // 3
    lane = lax.broadcasted_iota(jnp.int32, (nodes, samples), 1).astype(jnp.int16)
    nothing = jnp.zeros((), BF16)

    def part(e, c):
        return u[e * nodes : (e + 1) * nodes, c * samples : (c + 1) * samples]

    blocks = []
    for pair in range(0, GROUP, 2):
        sides = [jnp.concatenate([part(e, c) for c in range(3)], axis=0) for e in (pair, pair + 1)]
        product = dot(stiff, jnp.concatenate(sides, axis=1))
        for side, e in enumerate((pair, pair + 1)):
            k = stiff_coef_ref[first + e]
            m = mass_coef_ref[first + e]
            row = []
            for c in range(3):
                own = product[c * nodes : (c + 1) * nodes, side * samples : (side + 1) * samples]
                w = part(e, c)
                before = jnp.where(lane == 0, nothing, pltpu.roll(w, 1, 1))
                after = jnp.where(lane == samples - 1, nothing, pltpu.roll(w, samples - 1, 1))
                accel = ((before + after) - (w + w)).astype(F32)
                row.append((k * own + m * accel).astype(BF16))
            blocks.append(jnp.concatenate(row, axis=1))
    return jnp.concatenate(blocks, axis=0)


def chunks_of(ref, groups):
    rows = ref.shape[0] // groups
    return [ref.at[g * rows : (g + 1) * rows, :] for g in range(groups)]


def sweep(groups, gather, forces, add):
    for turn in range(groups + 2):
        if turn >= 2:
            add(turn - 2)
        if 1 <= turn <= groups:
            forces(turn - 1)
        if turn < groups:
            gather(turn)


def forces_stage(held, stiff_ref, coefs, force_chunks):
    def stage(group):
        force_chunks[group][...] = element_forces(
            held[group % 2][...], stiff_ref[...], *coefs, group * GROUP
        )

    return stage


def dam_first_kernel(
    free_hbm,
    dam_conn_hbm,
    dam_hbm,
    stiff_hbm,
    stiff_coef_hbm,
    mass_coef_hbm,
    back_hbm,
    order_hbm,
    force_hbm,
    free_made_hbm,
    dam_made_hbm,
    free_ref,
    dam_conn_ref,
    dam_ref,
    stiff_ref,
    stiff_coef_ref,
    mass_coef_ref,
    back_ref,
    force_ref,
    free_made,
    dam_made,
    held0,
    held1,
    sems,
    force_sems,
    free_sems,
    dam_sems,
):
    inward = transfer(
        [
            (free_hbm, free_ref),
            (dam_conn_hbm, dam_conn_ref),
            (dam_hbm, dam_ref),
            (stiff_hbm, stiff_ref),
            (stiff_coef_hbm, stiff_coef_ref),
            (mass_coef_hbm, mass_coef_ref),
        ],
        sems,
    )
    finish(inward)
    stiff_ref[...] = by_component(stiff_ref[...])
    outward = transfer([(stiff_ref, order_hbm)], sems)
    free_columns, dam_columns = free_ref[...].T, dam_conn_ref[...].T
    groups = dam_conn_ref.shape[0] // GROUP
    held = (held0, held1)
    force_chunks = chunks_of(force_ref, groups)
    free_chunks = chunks_of(free_made, groups)
    dam_chunks = chunks_of(dam_made, groups)

    def send(chunks, target, sems, group):
        copy = pltpu.make_async_copy(
            chunks[group], chunks_of(target, groups)[group], sems.at[group]
        )
        copy.start()
        outward.append(copy)

    def gather(group):
        select = select_rows(dam_columns, group * GROUP, dam_made.shape[1])
        dam_chunks[group][...] = select
        held[group % 2][...] = dot(select, dam_ref[...]).astype(BF16)

    def add(group):
        select = select_rows(free_columns, group * GROUP, free_made.shape[1])
        free_chunks[group][...] = select
        part = dot_first(force_chunks[group][...], select)
        back_ref[...] = part if group == 0 else back_ref[...] + part
        send(force_chunks, force_hbm, force_sems, group)
        send(dam_chunks, dam_made_hbm, dam_sems, group)
        send(free_chunks, free_made_hbm, free_sems, group)

    coefs = (stiff_coef_ref, mass_coef_ref)
    sweep(groups, gather, forces_stage(held, stiff_ref, coefs, force_chunks), add)
    finish(outward)
    finish(transfer([(back_ref, back_hbm)], sems))


def part_kernel(
    last,
    gather_hbm,
    add_hbm,
    table_ref,
    order_hbm,
    stiff_coef_hbm,
    mass_coef_hbm,
    *refs,
):
    if last:
        (start_hbm, force_hbm, out_hbm, start_ref, out_ref, *refs) = refs
        add_made, made_sems = None, refs[-2]
    else:
        (force_hbm, out_hbm, add_made, add_sems, *refs) = refs
        made_sems = refs[-2]
    order_ref, stiff_coef_ref, mass_coef_ref, total_ref, force_ref, made, held0, held1 = refs[:8]
    sems, made_sems, force_sems = refs[8:]
    groups = made_sems.shape[0]
    arriving = transfer(list(zip(chunks_of(gather_hbm, groups), chunks_of(made, groups))), made_sems)
    inward = transfer(
        [
            (order_hbm, order_ref),
            (stiff_coef_hbm, stiff_coef_ref),
            (mass_coef_hbm, mass_coef_ref),
        ],
        sems,
    )
    if last:
        starting = pltpu.make_async_copy(start_hbm, start_ref, sems.at[3])
        starting.start()
    else:
        adding = transfer(
            list(zip(chunks_of(add_hbm, groups), chunks_of(add_made, groups))), add_sems
        )
    outward = []
    held = (held0, held1)
    force_chunks = chunks_of(force_ref, groups)
    made_chunks = chunks_of(made, groups)
    add_chunks = made_chunks if last else chunks_of(add_made, groups)

    def gather(group):
        finish(arriving[group : group + 1])
        held[group % 2][...] = dot(made_chunks[group][...], table_ref[...]).astype(BF16)
        if group == 0:
            finish(inward)

    def add(group):
        if not last:
            finish(adding[group : group + 1])
        copy = pltpu.make_async_copy(
            force_chunks[group], chunks_of(force_hbm, groups)[group], force_sems.at[group]
        )
        copy.start()
        outward.append(copy)
        part = dot_first(force_chunks[group][...], add_chunks[group][...])
        total_ref[...] = part if group == 0 else total_ref[...] + part

    coefs = (stiff_coef_ref, mass_coef_ref)
    sweep(groups, gather, forces_stage(held, order_ref, coefs, force_chunks), add)
    if last:
        starting.wait()
        lanes = 128
        slots = total_ref.shape[1]
        for i, at in enumerate(range(0, slots, lanes)):
            part = start_ref[:, at : at + lanes] + total_ref[:, at : at + lanes]
            out_ref[at : at + lanes, :] = part.T.astype(BF16)
            copy = pltpu.make_async_copy(
                out_ref.at[at : at + lanes, :], out_hbm.at[at : at + lanes, :], sems.at[i % 4]
            )
            copy.start()
            outward.append(copy)
    else:
        outward += transfer([(total_ref, out_hbm)], sems)
    finish(outward)


def dam_update_kernel(
    made_hbm,
    free_force_hbm,
    dam_force_hbm,
    dam_hbm,
    step_hbm,
    next_hbm,
    made,
    free_force,
    dam_force,
    total_ref,
    dam_ref,
    step_ref,
    next_ref,
    sems,
    made_sems,
    free_sems,
    dam_sems,
):
    groups = made_sems.shape[0]

    def bring(source, target, sems):
        return transfer(list(zip(chunks_of(source, groups), chunks_of(target, groups))), sems)

    arriving = [
        bring(made_hbm, made, made_sems),
        bring(free_force_hbm, free_force, free_sems),
        bring(dam_force_hbm, dam_force, dam_sems),
    ]
    inward = transfer([(dam_hbm, dam_ref), (step_hbm, step_ref)], sems)
    for group in range(groups):
        finish([copies[group] for copies in arriving])
        force = chunks_of(free_force, groups)[group][...].astype(F32)
        force = (force + chunks_of(dam_force, groups)[group][...].astype(F32)).astype(BF16)
        part = dot_first(force, chunks_of(made, groups)[group][...])
        total_ref[...] = part if group == 0 else total_ref[...] + part
    finish(inward)
    step = as_column(step_ref[...])
    next_ref[...] = (dam_ref[...].astype(F32) - step * total_ref[...].T).astype(BF16)
    finish(transfer([(next_ref, next_hbm)], sems))


def exchange(rows, devices, capacity):
    width = rows.shape[1]
    shaped = rows.reshape(devices, capacity, width)
    arrived = lax.all_to_all(shaped, ("reg", "dam"), split_axis=0, concat_axis=0, tiled=True)
    return arrived.reshape(devices * capacity, width)


def kernel(body, name, n_in, outs, scratch, inside=(), flops=0, moved=0):
    hbm = pl.BlockSpec(memory_space=pltpu.HBM)
    vmem = pl.BlockSpec(memory_space=pltpu.VMEM)
    call = pl.pallas_call(
        body,
        name=name,
        in_specs=[vmem if i in inside else hbm for i in range(n_in)],
        out_specs=[hbm] * len(outs),
        out_shape=[pltpu.HBM(*out) for out in outs],
        scratch_shapes=scratch,
        compiler_params=pltpu.CompilerParams(vmem_limit_bytes=VMEM_BYTES),
        cost_estimate=pl.CostEstimate(flops=flops, bytes_accessed=moved, transcendentals=0),
    )

    def run(*operands):
        return call(
            *[
                x if i in inside else pltpu.with_memory_space_constraint(x, pltpu.HBM)
                for i, x in enumerate(operands)
            ]
        )

    return run


def shards(
    history,
    routes,
    dam_field,
    conn_free,
    conn_dam,
    stiff_ref,
    stiff_coef,
    mass_coef,
    reg_step,
    dam_step,
):
    devices = lax.axis_size(("reg", "dam"))
    row_count, width = history.shape
    capacity = 4 * row_count // devices
    slots = devices * capacity
    dam_count = dam_field.shape[0]
    elements, nodes = conn_free.shape
    all_pairs = elements * nodes
    pairs = GROUP * nodes
    groups = elements // GROUP

    I32 = jnp.int32
    vmem = pltpu.VMEM
    dma = pltpu.SemaphoreType.DMA
    conn = vmem((elements, nodes), I32)
    stiff = vmem(stiff_ref.shape, BF16)
    coefs = [pltpu.SMEM((elements,), F32)] * 2
    held = [vmem((pairs, width), BF16)] * 2
    forces_type = ((all_pairs, width), BF16)
    free_type = ((all_pairs, slots), BF16)
    dam_rows_type = ((all_pairs, dam_count), BF16)
    back_type = ((width, slots), F32)
    stiff_type = (stiff_ref.shape, BF16)
    place_type = ((slots, row_count), BF16)
    slots_type = ((slots, width), BF16)
    rows_type = ((row_count, width), BF16)
    dam_type = ((dam_count, width), BF16)
    product = 2 * all_pairs * slots * width

    pack = kernel(
        functools.partial(pack_kernel, capacity),
        "pack",
        2,
        [slots_type, place_type],
        [vmem((2, row_count), I32), vmem(*rows_type), vmem(*slots_type), vmem(*place_type), dma((2,))],
    )
    turn_scratch = [vmem(*place_type), vmem(*rows_type), vmem((1, row_count), F32), vmem(*rows_type)]
    turn = kernel(
        turn_kernel,
        "turn",
        5,
        [rows_type, slots_type],
        turn_scratch + [vmem(*slots_type), dma((3,))],
        inside=(1,),
    )
    last = kernel(
        last_kernel,
        "last",
        5,
        [rows_type, ((row_count, width), F32)],
        turn_scratch + [vmem((row_count, width), F32), dma((3,))],
        inside=(1,),
    )
    dam_first = kernel(
        dam_first_kernel,
        "dam_first",
        6,
        [back_type, stiff_type, forces_type, free_type, dam_rows_type],
        [conn, conn, vmem(*dam_type), stiff, *coefs]
        + [vmem(*back_type), vmem(*forces_type), vmem(*free_type), vmem(*dam_rows_type)]
        + [*held, dma((6,)), dma((groups,)), dma((groups,)), dma((groups,))],
        flops=3 * product,
        moved=4 * all_pairs * width,
    )
    part_scratch = [stiff, *coefs, vmem(*back_type), vmem(*forces_type)]
    part_sems = [dma((4,)), dma((groups,)), dma((groups,))]
    dam_again = kernel(
        functools.partial(part_kernel, False),
        "dam_again",
        6,
        [forces_type, back_type],
        [vmem(*free_type), dma((groups,))]
        + part_scratch
        + [vmem(*dam_rows_type), *held]
        + part_sems,
        inside=(2,),
        flops=3 * product,
        moved=4 * all_pairs * width,
    )
    free_part = kernel(
        functools.partial(part_kernel, True),
        "free_part",
        7,
        [forces_type, slots_type],
        [vmem(*back_type), vmem(*slots_type)]
        + part_scratch
        + [vmem(*free_type), *held]
        + part_sems,
        inside=(2,),
        flops=3 * product,
        moved=4 * all_pairs * width,
    )
    dam_update = kernel(
        dam_update_kernel,
        "dam_update",
        5,
        [dam_type],
        [vmem(*dam_rows_type), vmem(*forces_type), vmem(*forces_type)]
        + [vmem((width, dam_count), F32), vmem(*dam_type), vmem((1, dam_count), F32)]
        + [vmem(*dam_type), dma((2,)), dma((groups,)), dma((groups,)), dma((groups,))],
        flops=product,
        moved=4 * all_pairs * width,
    )

    reg_row = reg_step.reshape(1, row_count)
    dam_row = dam_step.reshape(1, dam_count)
    outgoing, place = pack(routes.T, history)
    for round_index in range(ROUNDS):
        received = exchange(outgoing, devices, capacity)
        if round_index == 0:
            back_start, ordered, dam_force, free_made, dam_made = dam_first(
                conn_free, conn_dam, dam_field, stiff_ref, stiff_coef, mass_coef
            )
        else:
            dam_force, back_start = dam_again(
                dam_made, free_made, dam_field, ordered, stiff_coef, mass_coef
            )
        free_force, back = free_part(
            free_made, free_made, received, ordered, stiff_coef, mass_coef, back_start
        )
        returned = exchange(back, devices, capacity)
        (dam_field,) = dam_update(dam_made, free_force, dam_force, dam_field, dam_row)
        if round_index < ROUNDS - 1:
            history, outgoing = turn(place, returned, history, reg_row, dam_field)
        else:
            history, pulled = last(place, returned, history, reg_row, dam_field)
    return (history, pulled, dam_field)


def solution(mesh):
    rows = P(("reg", "dam"), None)
    flat = P(("reg", "dam"))
    in_specs = (rows, rows, rows, rows, rows, P(), flat, flat, flat, flat)
    return jax.shard_map(
        shards, mesh=mesh, in_specs=in_specs, out_specs=(rows, rows, rows), check_vma=False
    )
```

```python
import functools

import jax
import jax.numpy as jnp
from jax import lax
from jax.experimental import pallas as pl
from jax.experimental.pallas import tpu as pltpu
from jax.sharding import PartitionSpec as P

ROUNDS = 2
GROUP = 8
VMEM_BYTES = 28 * 1024 * 1024
BF16 = jnp.bfloat16
F32 = jnp.float32


def mask_to_bf16(mask):
    return jnp.where(mask, 1.0, 0.0).astype(BF16)


def dot(left, right):
    return jnp.dot(left, right, preferred_element_type=F32)


def dot_first(left, right):
    return lax.dot_general(left, right, (((0,), (0,)), ((), ())), preferred_element_type=F32)


def transfer(pairs, sems):
    copies = [pltpu.make_async_copy(a, b, sems.at[i]) for i, (a, b) in enumerate(pairs)]
    for copy in copies:
        copy.start()
    return copies


def finish(copies):
    for copy in copies:
        copy.wait()


def as_column(row):
    size = row.shape[1]
    down = lax.broadcasted_iota(jnp.int32, (size, size), 0)
    across = lax.broadcasted_iota(jnp.int32, (size, size), 1)
    return jnp.sum(jnp.where(down == across, row, jnp.zeros_like(row)), axis=1, keepdims=True)


def pack_kernel(
    capacity, routes_hbm, history_hbm, out_hbm, place_hbm, routes_ref, history_ref, out_ref, place_ref, sems
):
    inward = transfer([(routes_hbm, routes_ref), (history_hbm, history_ref)], sems)
    slots, rows = place_ref.shape
    finish(inward[:1])
    row0, row1 = routes_ref[0:1, :], routes_ref[1:2, :]
    col0, col1 = as_column(row0), as_column(row1)
    down = lax.broadcasted_iota(jnp.int32, (rows, rows), 0)
    across = lax.broadcasted_iota(jnp.int32, (rows, rows), 1)
    numbers = lax.broadcasted_iota(jnp.int32, (slots, rows), 0)
    hits = []
    for own in (row0, row1):
        same = jnp.where(col0 == own, 1, 0) + jnp.where(col1 == own, 1, 0)
        slot = jnp.sum(jnp.where(down < across, same, 0), axis=0, keepdims=True)
        hits.append(own * capacity + slot == numbers)
    place = mask_to_bf16(hits[0] | hits[1])
    place_ref[...] = place
    finish(inward[1:])
    out_ref[...] = dot(place, history_ref[...]).astype(BF16)
    finish(transfer([(out_ref, out_hbm), (place_ref, place_hbm)], sems))


def turn_kernel(
    place_hbm,
    returned_ref,
    history_hbm,
    step_hbm,
    after_hbm,
    next_hbm,
    out_hbm,
    place_ref,
    history_ref,
    step_ref,
    next_ref,
    out_ref,
    sems,
):
    inward = transfer(
        [(place_hbm, place_ref), (history_hbm, history_ref), (step_hbm, step_ref)], sems
    )
    finish(inward)
    place = place_ref[...]
    pulled = dot_first(place, returned_ref[...])
    step = as_column(step_ref[...])
    following = (history_ref[...].astype(F32) - step * pulled).astype(BF16)
    next_ref[...] = following
    out_ref[...] = dot(place, following).astype(BF16)
    finish(transfer([(next_ref, next_hbm), (out_ref, out_hbm)], sems))


def last_kernel(
    place_hbm,
    returned_ref,
    history_hbm,
    step_hbm,
    after_hbm,
    next_hbm,
    pulled_hbm,
    place_ref,
    history_ref,
    step_ref,
    next_ref,
    pulled_ref,
    sems,
):
    inward = transfer(
        [(place_hbm, place_ref), (history_hbm, history_ref), (step_hbm, step_ref)], sems
    )
    finish(inward)
    pulled = dot_first(place_ref[...], returned_ref[...])
    step = as_column(step_ref[...])
    next_ref[...] = (history_ref[...].astype(F32) - step * pulled).astype(BF16)
    pulled_ref[...] = pulled
    finish(transfer([(next_ref, next_hbm), (pulled_ref, pulled_hbm)], sems))


def by_component(stiff):
    size = stiff.shape[0]
    nodes = size // 3
    down = lax.broadcasted_iota(jnp.int32, (size, size), 0)
    across = lax.broadcasted_iota(jnp.int32, (size, size), 1)
    part = (down >= nodes).astype(jnp.int32) + (down >= 2 * nodes).astype(jnp.int32)
    order = mask_to_bf16(across == 3 * (down - part * nodes) + part)
    half = dot(order, stiff).astype(BF16)
    return lax.dot_general(
        half, order, (((1,), (1,)), ((), ())), preferred_element_type=F32
    ).astype(BF16)


def select_rows(columns, first, width):
    nodes = columns.shape[0]
    lanes = lax.broadcasted_iota(jnp.int32, (nodes, width), 1).astype(jnp.int16)
    parts = []
    for e in range(first, first + GROUP):
        own = jnp.broadcast_to(columns[:, e : e + 1], (nodes, width)).astype(jnp.int16)
        parts.append(jnp.where(own == lanes, jnp.ones((), BF16), jnp.zeros((), BF16)))
    return jnp.concatenate(parts, axis=0)


def element_forces(u, stiff, stiff_coef_ref, mass_coef_ref, first):
    nodes = u.shape[0] // GROUP
    samples = u.shape[1] // 3
    lane = lax.broadcasted_iota(jnp.int32, (nodes, samples), 1).astype(jnp.int16)
    nothing = jnp.zeros((), BF16)

    def part(e, c):
        return u[e * nodes : (e + 1) * nodes, c * samples : (c + 1) * samples]

    blocks = []
    for pair in range(0, GROUP, 2):
        sides = [jnp.concatenate([part(e, c) for c in range(3)], axis=0) for e in (pair, pair + 1)]
        product = dot(stiff, jnp.concatenate(sides, axis=1))
        for side, e in enumerate((pair, pair + 1)):
            k = stiff_coef_ref[first + e]
            m = mass_coef_ref[first + e]
            row = []
            for c in range(3):
                own = product[c * nodes : (c + 1) * nodes, side * samples : (side + 1) * samples]
                w = part(e, c)
                before = jnp.where(lane == 0, nothing, pltpu.roll(w, 1, 1))
                after = jnp.where(lane == samples - 1, nothing, pltpu.roll(w, samples - 1, 1))
                accel = ((before + after) - (w + w)).astype(F32)
                row.append((k * own + m * accel).astype(BF16))
            blocks.append(jnp.concatenate(row, axis=1))
    return jnp.concatenate(blocks, axis=0)


def chunks_of(ref, groups):
    rows = ref.shape[0] // groups
    return [ref.at[g * rows : (g + 1) * rows, :] for g in range(groups)]


def sweep(groups, gather, forces, add):
    for turn in range(groups + 2):
        if turn >= 2:
            add(turn - 2)
        if 1 <= turn <= groups:
            forces(turn - 1)
        if turn < groups:
            gather(turn)


def forces_stage(held, stiff_ref, coefs, force_chunks):
    def stage(group):
        force_chunks[group][...] = element_forces(
            held[group % 2][...], stiff_ref[...], *coefs, group * GROUP
        )

    return stage


class Sender:
    def __init__(self, source, target, sems):
        self.chunks = chunks_of(source, sems.shape[0])
        self.targets = chunks_of(target, sems.shape[0])
        self.sems = sems
        self.started = []

    def start(self, group):
        copy = pltpu.make_async_copy(self.chunks[group], self.targets[group], self.sems.at[group])
        copy.start()
        self.started.append(copy)

    def finish(self):
        finish(self.started)


def dam_part_kernel(
    free_hbm,
    dam_conn_hbm,
    dam_hbm,
    stiff_hbm,
    stiff_coef_hbm,
    mass_coef_hbm,
    back_hbm,
    order_hbm,
    force_hbm,
    free_ref,
    dam_conn_ref,
    dam_ref,
    stiff_ref,
    stiff_coef_ref,
    mass_coef_ref,
    back_ref,
    force_ref,
    held0,
    held1,
    sems,
    force_sems,
):
    inward = transfer(
        [
            (dam_conn_hbm, dam_conn_ref),
            (dam_hbm, dam_ref),
            (stiff_hbm, stiff_ref),
            (free_hbm, free_ref),
            (stiff_coef_hbm, stiff_coef_ref),
            (mass_coef_hbm, mass_coef_ref),
        ],
        sems,
    )
    finish(inward)
    stiff_ref[...] = by_component(stiff_ref[...])
    outward = transfer([(stiff_ref, order_hbm)], sems)
    free_columns, dam_columns = free_ref[...].T, dam_conn_ref[...].T
    groups = force_sems.shape[0]
    held = (held0, held1)
    sender = Sender(force_ref, force_hbm, force_sems)

    def gather(group):
        select = select_rows(dam_columns, group * GROUP, dam_ref.shape[0])
        held[group % 2][...] = dot(select, dam_ref[...]).astype(BF16)

    def add(group):
        sender.start(group)
        select = select_rows(free_columns, group * GROUP, back_ref.shape[1])
        part = dot_first(sender.chunks[group][...], select)
        back_ref[...] = part if group == 0 else back_ref[...] + part

    coefs = (stiff_coef_ref, mass_coef_ref)
    sweep(groups, gather, forces_stage(held, stiff_ref, coefs, sender.chunks), add)
    finish(outward)
    finish(transfer([(back_ref, back_hbm)], sems))
    sender.finish()


def free_part_kernel(
    free_hbm,
    received_ref,
    order_hbm,
    stiff_coef_hbm,
    mass_coef_hbm,
    start_hbm,
    force_hbm,
    back_hbm,
    free_ref,
    order_ref,
    stiff_coef_ref,
    mass_coef_ref,
    start_ref,
    total_ref,
    made,
    force_ref,
    back_ref,
    held0,
    held1,
    sems,
    force_sems,
):
    inward = transfer(
        [
            (free_hbm, free_ref),
            (order_hbm, order_ref),
            (stiff_coef_hbm, stiff_coef_ref),
            (mass_coef_hbm, mass_coef_ref),
            (start_hbm, start_ref),
        ],
        sems,
    )
    finish(inward[:1])
    columns = free_ref[...].T
    groups = force_sems.shape[0]
    made_chunks = chunks_of(made, groups)
    held = (held0, held1)
    sender = Sender(force_ref, force_hbm, force_sems)

    def gather(group):
        select = select_rows(columns, group * GROUP, received_ref.shape[0])
        made_chunks[group][...] = select
        held[group % 2][...] = dot(select, received_ref[...]).astype(BF16)
        if group == 0:
            finish(inward[1:4])

    def add(group):
        sender.start(group)
        part = dot_first(sender.chunks[group][...], made_chunks[group][...])
        total_ref[...] = part if group == 0 else total_ref[...] + part

    coefs = (stiff_coef_ref, mass_coef_ref)
    sweep(groups, gather, forces_stage(held, order_ref, coefs, sender.chunks), add)
    finish(inward[4:])
    slots = total_ref.shape[1]
    quarter = slots // 4
    outward = []
    for i in range(4):
        rows = slice(i * quarter, (i + 1) * quarter)
        back_ref[rows, :] = (start_ref[:, rows] + total_ref[:, rows]).T.astype(BF16)
        copy = pltpu.make_async_copy(back_ref.at[rows, :], back_hbm.at[rows, :], sems.at[i])
        copy.start()
        outward.append(copy)
    finish(outward)
    sender.finish()


def dam_update_kernel(
    dam_conn_hbm,
    free_force_hbm,
    dam_force_hbm,
    dam_hbm,
    step_hbm,
    next_hbm,
    dam_conn_ref,
    free_force,
    dam_force,
    total_ref,
    dam_ref,
    step_ref,
    next_ref,
    sems,
    free_sems,
    dam_sems,
):
    groups = free_sems.shape[0]
    inward = transfer([(dam_conn_hbm, dam_conn_ref), (dam_hbm, dam_ref), (step_hbm, step_ref)], sems)
    free_chunks, dam_chunks = chunks_of(free_force, groups), chunks_of(dam_force, groups)
    free_copies = transfer(list(zip(chunks_of(free_force_hbm, groups), free_chunks)), free_sems)
    dam_copies = transfer(list(zip(chunks_of(dam_force_hbm, groups), dam_chunks)), dam_sems)
    finish(inward)
    columns = dam_conn_ref[...].T
    for group in range(groups):
        finish([free_copies[group], dam_copies[group]])
        force = free_chunks[group][...].astype(F32) + dam_chunks[group][...].astype(F32)
        select = select_rows(columns, group * GROUP, dam_ref.shape[0])
        part = dot_first(force.astype(BF16), select)
        total_ref[...] = part if group == 0 else total_ref[...] + part
    step = as_column(step_ref[...])
    next_ref[...] = (dam_ref[...].astype(F32) - step * total_ref[...].T).astype(BF16)
    finish(transfer([(next_ref, next_hbm)], sems))


def exchange(rows, devices, capacity):
    width = rows.shape[1]
    shaped = rows.reshape(devices, capacity, width)
    arrived = lax.all_to_all(shaped, ("reg", "dam"), split_axis=0, concat_axis=0, tiled=True)
    return arrived.reshape(devices * capacity, width)


def kernel(body, name, n_in, outs, scratch, inside=(), flops=0, moved=0):
    hbm = pl.BlockSpec(memory_space=pltpu.HBM)
    vmem = pl.BlockSpec(memory_space=pltpu.VMEM)
    call = pl.pallas_call(
        body,
        name=name,
        in_specs=[vmem if i in inside else hbm for i in range(n_in)],
        out_specs=[hbm] * len(outs),
        out_shape=[pltpu.HBM(*out) for out in outs],
        scratch_shapes=scratch,
        compiler_params=pltpu.CompilerParams(vmem_limit_bytes=VMEM_BYTES),
        cost_estimate=pl.CostEstimate(flops=flops, bytes_accessed=moved, transcendentals=0),
    )

    def run(*operands):
        return call(
            *[
                x if i in inside else pltpu.with_memory_space_constraint(x, pltpu.HBM)
                for i, x in enumerate(operands)
            ]
        )

    return run


def shards(
    history,
    routes,
    dam_field,
    conn_free,
    conn_dam,
    stiff_ref,
    stiff_coef,
    mass_coef,
    reg_step,
    dam_step,
):
    devices = lax.axis_size(("reg", "dam"))
    row_count, width = history.shape
    capacity = 4 * row_count // devices
    slots = devices * capacity
    dam_count = dam_field.shape[0]
    elements, nodes = conn_free.shape
    all_pairs = elements * nodes
    pairs = GROUP * nodes
    groups = elements // GROUP

    I32 = jnp.int32
    vmem = pltpu.VMEM
    dma = pltpu.SemaphoreType.DMA
    conn = vmem((elements, nodes), I32)
    stiff = vmem(stiff_ref.shape, BF16)
    coefs = [pltpu.SMEM((elements,), F32)] * 2
    held = [vmem((pairs, width), BF16)] * 2
    forces_type = ((all_pairs, width), BF16)
    free_type = ((all_pairs, slots), BF16)
    back_type = ((width, slots), F32)
    stiff_type = (stiff_ref.shape, BF16)
    place_type = ((slots, row_count), BF16)
    slots_type = ((slots, width), BF16)
    rows_type = ((row_count, width), BF16)
    dam_type = ((dam_count, width), BF16)
    product = 2 * all_pairs * slots * width

    pack = kernel(
        functools.partial(pack_kernel, capacity),
        "pack",
        2,
        [slots_type, place_type],
        [vmem((2, row_count), I32), vmem(*rows_type), vmem(*slots_type), vmem(*place_type), dma((2,))],
    )
    turn_scratch = [vmem(*place_type), vmem(*rows_type), vmem((1, row_count), F32), vmem(*rows_type)]
    turn = kernel(
        turn_kernel,
        "turn",
        5,
        [rows_type, slots_type],
        turn_scratch + [vmem(*slots_type), dma((3,))],
        inside=(1,),
    )
    last = kernel(
        last_kernel,
        "last",
        5,
        [rows_type, ((row_count, width), F32)],
        turn_scratch + [vmem((row_count, width), F32), dma((3,))],
        inside=(1,),
    )
    dam_part = kernel(
        dam_part_kernel,
        "dam_part",
        6,
        [back_type, stiff_type, forces_type],
        [conn, conn, vmem(*dam_type), stiff, *coefs, vmem(*back_type), vmem(*forces_type)]
        + [*held, dma((6,)), dma((groups,))],
        flops=3 * product,
        moved=4 * all_pairs * width,
    )
    free_part = kernel(
        free_part_kernel,
        "free_part",
        6,
        [forces_type, slots_type],
        [conn, stiff, *coefs, vmem(*back_type), vmem(*back_type)]
        + [vmem(*free_type), vmem(*forces_type), vmem(*slots_type), *held]
        + [dma((5,)), dma((groups,))],
        inside=(1,),
        flops=3 * product,
        moved=4 * all_pairs * width,
    )
    dam_update = kernel(
        dam_update_kernel,
        "dam_update",
        5,
        [dam_type],
        [conn, vmem(*forces_type), vmem(*forces_type)]
        + [vmem((width, dam_count), F32), vmem(*dam_type), vmem((1, dam_count), F32)]
        + [vmem(*dam_type), dma((3,)), dma((groups,)), dma((groups,))],
        flops=product,
        moved=4 * all_pairs * width,
    )

    reg_row = reg_step.reshape(1, row_count)
    dam_row = dam_step.reshape(1, dam_count)
    outgoing, place = pack(routes.T, history)
    for round_index in range(ROUNDS):
        received = exchange(outgoing, devices, capacity)
        back_start, ordered, dam_force = dam_part(
            conn_free, conn_dam, dam_field, stiff_ref, stiff_coef, mass_coef
        )
        free_force, back = free_part(
            conn_free, received, ordered, stiff_coef, mass_coef, back_start
        )
        returned = exchange(back, devices, capacity)
        (dam_field,) = dam_update(conn_dam, free_force, dam_force, dam_field, dam_row)
        if round_index < ROUNDS - 1:
            history, outgoing = turn(place, returned, history, reg_row, dam_field)
        else:
            history, pulled = last(place, returned, history, reg_row, dam_field)
    return (history, pulled, dam_field)


def solution(mesh):
    rows = P(("reg", "dam"), None)
    flat = P(("reg", "dam"))
    in_specs = (rows, rows, rows, rows, rows, P(), flat, flat, flat, flat)
    return jax.shard_map(
        shards, mesh=mesh, in_specs=in_specs, out_specs=(rows, rows, rows), check_vma=False
    )
```

```python
import functools

import jax
import jax.numpy as jnp
from jax import lax
from jax.experimental import pallas as pl
from jax.experimental.pallas import tpu as pltpu
from jax.sharding import PartitionSpec as P

ROUNDS = 2
GROUP = 8
VMEM_BYTES = 28 * 1024 * 1024
BF16 = jnp.bfloat16
F32 = jnp.float32


def mask_to_bf16(mask):
    return jnp.where(mask, 1.0, 0.0).astype(BF16)


def dot(left, right):
    return jnp.dot(left, right, preferred_element_type=F32)


def dot_first(left, right):
    return lax.dot_general(left, right, (((0,), (0,)), ((), ())), preferred_element_type=F32)


def transfer(pairs, sems):
    copies = [pltpu.make_async_copy(a, b, sems.at[i]) for i, (a, b) in enumerate(pairs)]
    for copy in copies:
        copy.start()
    return copies


def finish(copies):
    for copy in copies:
        copy.wait()


def as_column(row):
    size = row.shape[1]
    down = lax.broadcasted_iota(jnp.int32, (size, size), 0)
    across = lax.broadcasted_iota(jnp.int32, (size, size), 1)
    return jnp.sum(jnp.where(down == across, row, jnp.zeros_like(row)), axis=1, keepdims=True)


def pack_kernel(
    capacity,
    routes_hbm,
    history_hbm,
    step_hbm,
    out_hbm,
    place_ref,
    history_ref,
    column_ref,
    routes_ref,
    step_ref,
    out_ref,
    sems,
):
    inward = transfer(
        [(routes_hbm, routes_ref), (history_hbm, history_ref), (step_hbm, step_ref)], sems
    )
    slots, rows = place_ref.shape
    finish(inward[:1])
    row0, row1 = routes_ref[0:1, :], routes_ref[1:2, :]
    col0, col1 = as_column(row0), as_column(row1)
    down = lax.broadcasted_iota(jnp.int32, (rows, rows), 0)
    across = lax.broadcasted_iota(jnp.int32, (rows, rows), 1)
    numbers = lax.broadcasted_iota(jnp.int32, (slots, rows), 0)
    hits = []
    for own in (row0, row1):
        same = jnp.where(col0 == own, 1, 0) + jnp.where(col1 == own, 1, 0)
        slot = jnp.sum(jnp.where(down < across, same, 0), axis=0, keepdims=True)
        hits.append(own * capacity + slot == numbers)
    place = mask_to_bf16(hits[0] | hits[1])
    place_ref[...] = place
    finish(inward[1:])
    out_ref[...] = dot(place, history_ref[...]).astype(BF16)
    outward = transfer([(out_ref, out_hbm)], sems)
    column_ref[...] = jnp.broadcast_to(as_column(step_ref[...]), column_ref.shape)
    finish(outward)


def turn_kernel(
    place_ref, returned_ref, history_ref, column_ref, after_hbm, next_ref, out_hbm, out_ref, sems
):
    place = place_ref[...]
    pulled = dot_first(place, returned_ref[...])
    following = (history_ref[...].astype(F32) - column_ref[:, 0:1] * pulled).astype(BF16)
    next_ref[...] = following
    out_ref[...] = dot(place, following).astype(BF16)
    finish(transfer([(out_ref, out_hbm)], sems))


def last_kernel(
    place_ref,
    returned_ref,
    history_ref,
    column_ref,
    after_hbm,
    next_hbm,
    pulled_hbm,
    next_ref,
    pulled_ref,
    sems,
):
    pulled = dot_first(place_ref[...], returned_ref[...])
    pulled_ref[...] = pulled
    outward = transfer([(pulled_ref, pulled_hbm)], sems)
    next_ref[...] = (history_ref[...].astype(F32) - column_ref[:, 0:1] * pulled).astype(BF16)
    finish(outward + transfer([(next_ref, next_hbm)], sems.at[1:2]))


def by_component(stiff):
    size = stiff.shape[0]
    nodes = size // 3
    down = lax.broadcasted_iota(jnp.int32, (size, size), 0)
    across = lax.broadcasted_iota(jnp.int32, (size, size), 1)
    part = (down >= nodes).astype(jnp.int32) + (down >= 2 * nodes).astype(jnp.int32)
    order = mask_to_bf16(across == 3 * (down - part * nodes) + part)
    half = dot(order, stiff).astype(BF16)
    return lax.dot_general(
        half, order, (((1,), (1,)), ((), ())), preferred_element_type=F32
    ).astype(BF16)


def select_rows(columns, first, width):
    nodes = columns.shape[0]
    lanes = lax.broadcasted_iota(jnp.int32, (nodes, width), 1).astype(jnp.int16)
    parts = []
    for e in range(first, first + GROUP):
        own = jnp.broadcast_to(columns[:, e : e + 1], (nodes, width)).astype(jnp.int16)
        parts.append(jnp.where(own == lanes, jnp.ones((), BF16), jnp.zeros((), BF16)))
    return jnp.concatenate(parts, axis=0)


def element_forces(u, stiff, stiff_coef_ref, mass_coef_ref, first):
    nodes = u.shape[0] // GROUP
    samples = u.shape[1] // 3
    lane = lax.broadcasted_iota(jnp.int32, (nodes, samples), 1).astype(jnp.int16)
    nothing = jnp.zeros((), BF16)

    def part(e, c):
        return u[e * nodes : (e + 1) * nodes, c * samples : (c + 1) * samples]

    blocks = []
    for pair in range(0, GROUP, 2):
        sides = [jnp.concatenate([part(e, c) for c in range(3)], axis=0) for e in (pair, pair + 1)]
        product = dot(stiff, jnp.concatenate(sides, axis=1))
        for side, e in enumerate((pair, pair + 1)):
            k = stiff_coef_ref[first + e]
            m = mass_coef_ref[first + e]
            row = []
            for c in range(3):
                own = product[c * nodes : (c + 1) * nodes, side * samples : (side + 1) * samples]
                w = part(e, c)
                before = jnp.where(lane == 0, nothing, pltpu.roll(w, 1, 1))
                after = jnp.where(lane == samples - 1, nothing, pltpu.roll(w, samples - 1, 1))
                accel = ((before + after) - (w + w)).astype(F32)
                row.append((k * own + m * accel).astype(BF16))
            blocks.append(jnp.concatenate(row, axis=1))
    return jnp.concatenate(blocks, axis=0)


def chunks_of(ref, groups):
    rows = ref.shape[0] // groups
    return [ref.at[g * rows : (g + 1) * rows, :] for g in range(groups)]


def sweep(groups, gather, forces, add):
    for turn in range(groups + 2):
        if turn >= 2:
            add(turn - 2)
        if 1 <= turn <= groups:
            forces(turn - 1)
        if turn < groups:
            gather(turn)


def forces_stage(held, stiff_ref, coefs, force_chunks):
    def stage(group):
        force_chunks[group][...] = element_forces(
            held[group % 2][...], stiff_ref[...], *coefs, group * GROUP
        )

    return stage


class Sender:
    def __init__(self, source, target, sems):
        self.chunks = chunks_of(source, sems.shape[0])
        self.targets = chunks_of(target, sems.shape[0])
        self.sems = sems
        self.started = []

    def start(self, group):
        copy = pltpu.make_async_copy(self.chunks[group], self.targets[group], self.sems.at[group])
        copy.start()
        self.started.append(copy)

    def finish(self):
        finish(self.started)


def dam_part_kernel(
    free_hbm,
    dam_conn_hbm,
    dam_hbm,
    stiff_hbm,
    stiff_coef_hbm,
    mass_coef_hbm,
    back_hbm,
    order_ref,
    columns_ref,
    force_hbm,
    free_ref,
    dam_conn_ref,
    dam_ref,
    stiff_ref,
    stiff_coef_ref,
    mass_coef_ref,
    back_ref,
    force_ref,
    held0,
    held1,
    sems,
    force_sems,
):
    inward = transfer(
        [
            (dam_conn_hbm, dam_conn_ref),
            (dam_hbm, dam_ref),
            (stiff_hbm, stiff_ref),
            (free_hbm, free_ref),
            (stiff_coef_hbm, stiff_coef_ref),
            (mass_coef_hbm, mass_coef_ref),
        ],
        sems,
    )
    finish(inward)
    order_ref[...] = by_component(stiff_ref[...])
    free_columns, dam_columns = free_ref[...].T, dam_conn_ref[...].T
    columns_ref[...] = free_columns
    groups = force_sems.shape[0]
    held = (held0, held1)
    sender = Sender(force_ref, force_hbm, force_sems)

    def gather(group):
        select = select_rows(dam_columns, group * GROUP, dam_ref.shape[0])
        held[group % 2][...] = dot(select, dam_ref[...]).astype(BF16)

    def add(group):
        sender.start(group)
        select = select_rows(free_columns, group * GROUP, back_ref.shape[1])
        part = dot_first(sender.chunks[group][...], select)
        back_ref[...] = part if group == 0 else back_ref[...] + part

    coefs = (stiff_coef_ref, mass_coef_ref)
    sweep(groups, gather, forces_stage(held, order_ref, coefs, sender.chunks), add)
    finish(transfer([(back_ref, back_hbm)], sems))
    sender.finish()


def free_part_kernel(
    columns_ref,
    received_ref,
    order_ref,
    stiff_coef_hbm,
    mass_coef_hbm,
    start_hbm,
    force_hbm,
    back_hbm,
    stiff_coef_ref,
    mass_coef_ref,
    start_ref,
    total_ref,
    made,
    force_ref,
    back_ref,
    held0,
    held1,
    sems,
    force_sems,
):
    inward = transfer(
        [
            (stiff_coef_hbm, stiff_coef_ref),
            (mass_coef_hbm, mass_coef_ref),
            (start_hbm, start_ref),
        ],
        sems,
    )
    columns = columns_ref[...]
    groups = force_sems.shape[0]
    made_chunks = chunks_of(made, groups)
    held = (held0, held1)
    sender = Sender(force_ref, force_hbm, force_sems)

    def gather(group):
        select = select_rows(columns, group * GROUP, received_ref.shape[0])
        made_chunks[group][...] = select
        held[group % 2][...] = dot(select, received_ref[...]).astype(BF16)
        if group == 0:
            finish(inward[:2])

    def add(group):
        sender.start(group)
        part = dot_first(sender.chunks[group][...], made_chunks[group][...])
        total_ref[...] = part if group == 0 else total_ref[...] + part

    coefs = (stiff_coef_ref, mass_coef_ref)
    sweep(groups, gather, forces_stage(held, order_ref, coefs, sender.chunks), add)
    finish(inward[2:])
    slots = total_ref.shape[1]
    quarter = slots // 4
    outward = []
    for i in range(4):
        rows = slice(i * quarter, (i + 1) * quarter)
        back_ref[rows, :] = (start_ref[:, rows] + total_ref[:, rows]).T.astype(BF16)
        copy = pltpu.make_async_copy(back_ref.at[rows, :], back_hbm.at[rows, :], sems.at[i])
        copy.start()
        outward.append(copy)
    finish(outward)
    sender.finish()


def dam_update_kernel(
    dam_conn_hbm,
    free_force_hbm,
    dam_force_hbm,
    dam_hbm,
    step_hbm,
    next_hbm,
    dam_conn_ref,
    free_force,
    dam_force,
    total_ref,
    dam_ref,
    step_ref,
    next_ref,
    sems,
    free_sems,
    dam_sems,
):
    groups = free_sems.shape[0]
    inward = transfer([(dam_conn_hbm, dam_conn_ref), (dam_hbm, dam_ref), (step_hbm, step_ref)], sems)
    free_chunks, dam_chunks = chunks_of(free_force, groups), chunks_of(dam_force, groups)
    free_copies = transfer(list(zip(chunks_of(free_force_hbm, groups), free_chunks)), free_sems)
    dam_copies = transfer(list(zip(chunks_of(dam_force_hbm, groups), dam_chunks)), dam_sems)
    finish(inward)
    columns = dam_conn_ref[...].T
    for group in range(groups):
        finish([free_copies[group], dam_copies[group]])
        force = free_chunks[group][...].astype(F32) + dam_chunks[group][...].astype(F32)
        select = select_rows(columns, group * GROUP, dam_ref.shape[0])
        part = dot_first(force.astype(BF16), select)
        total_ref[...] = part if group == 0 else total_ref[...] + part
    step = as_column(step_ref[...])
    next_ref[...] = (dam_ref[...].astype(F32) - step * total_ref[...].T).astype(BF16)
    finish(transfer([(next_ref, next_hbm)], sems))


def exchange(rows, devices, capacity):
    width = rows.shape[1]
    shaped = rows.reshape(devices, capacity, width)
    arrived = lax.all_to_all(shaped, ("reg", "dam"), split_axis=0, concat_axis=0, tiled=True)
    return arrived.reshape(devices * capacity, width)


def kernel(body, name, ins, outs, scratch, flops=0, moved=0):
    hbm = pl.BlockSpec(memory_space=pltpu.HBM)
    vmem = pl.BlockSpec(memory_space=pltpu.VMEM)
    spaces = {"h": pltpu.HBM, "v": pltpu.VMEM}
    call = pl.pallas_call(
        body,
        name=name,
        in_specs=[hbm if letter == "h" else vmem for letter in ins],
        out_specs=[hbm if out[0] == "h" else vmem for out in outs],
        out_shape=[spaces[out[0]](*out[1:]) for out in outs],
        scratch_shapes=scratch,
        compiler_params=pltpu.CompilerParams(vmem_limit_bytes=VMEM_BYTES),
        cost_estimate=pl.CostEstimate(flops=flops, bytes_accessed=moved, transcendentals=0),
    )

    def run(*operands):
        return call(
            *[
                x if letter == "a" else pltpu.with_memory_space_constraint(x, spaces[letter])
                for letter, x in zip(ins, operands)
            ]
        )

    return run


def shards(
    history,
    routes,
    dam_field,
    conn_free,
    conn_dam,
    stiff_ref,
    stiff_coef,
    mass_coef,
    reg_step,
    dam_step,
):
    devices = lax.axis_size(("reg", "dam"))
    row_count, width = history.shape
    capacity = 4 * row_count // devices
    slots = devices * capacity
    dam_count = dam_field.shape[0]
    elements, nodes = conn_free.shape
    all_pairs = elements * nodes
    pairs = GROUP * nodes
    groups = elements // GROUP

    I32 = jnp.int32
    vmem = pltpu.VMEM
    dma = pltpu.SemaphoreType.DMA
    conn = vmem((elements, nodes), I32)
    stiff = vmem(stiff_ref.shape, BF16)
    coefs = [pltpu.SMEM((elements,), F32)] * 2
    held = [vmem((pairs, width), BF16)] * 2
    forces_type = ((all_pairs, width), BF16)
    free_type = ((all_pairs, slots), BF16)
    back_type = ((width, slots), F32)
    stiff_type = (stiff_ref.shape, BF16)
    place_type = ((slots, row_count), BF16)
    slots_type = ((slots, width), BF16)
    rows_type = ((row_count, width), BF16)
    pulled_type = ((row_count, width), F32)
    column_type = ((row_count, 128), F32)
    dam_type = ((dam_count, width), BF16)
    product = 2 * all_pairs * slots * width

    pack = kernel(
        functools.partial(pack_kernel, capacity),
        "pack",
        "hhh",
        [("h", *slots_type), ("v", *place_type), ("v", *rows_type), ("v", *column_type)],
        [vmem((2, row_count), I32), vmem((1, row_count), F32), vmem(*slots_type), dma((3,))],
    )
    turn = kernel(
        turn_kernel,
        "turn",
        "vavvh",
        [("v", *rows_type), ("h", *slots_type)],
        [vmem(*slots_type), dma((1,))],
    )
    last = kernel(
        last_kernel,
        "last",
        "vavvh",
        [("h", *rows_type), ("h", *pulled_type)],
        [vmem(*rows_type), vmem(*pulled_type), dma((2,))],
    )
    dam_part = kernel(
        dam_part_kernel,
        "dam_part",
        "hhhhhh",
        [("h", *back_type), ("v", *stiff_type), ("v", (nodes, elements), I32), ("h", *forces_type)],
        [conn, conn, vmem(*dam_type), stiff, *coefs, vmem(*back_type), vmem(*forces_type)]
        + [*held, dma((6,)), dma((groups,))],
        flops=3 * product,
        moved=4 * all_pairs * width,
    )
    free_part = kernel(
        free_part_kernel,
        "free_part",
        "vavhhh",
        [("h", *forces_type), ("h", *slots_type)],
        [*coefs, vmem(*back_type), vmem(*back_type)]
        + [vmem(*free_type), vmem(*forces_type), vmem(*slots_type), *held]
        + [dma((4,)), dma((groups,))],
        flops=3 * product,
        moved=4 * all_pairs * width,
    )
    dam_update = kernel(
        dam_update_kernel,
        "dam_update",
        "hhhhh",
        [("h", *dam_type)],
        [conn, vmem(*forces_type), vmem(*forces_type)]
        + [vmem((width, dam_count), F32), vmem(*dam_type), vmem((1, dam_count), F32)]
        + [vmem(*dam_type), dma((3,)), dma((groups,)), dma((groups,))],
        flops=product,
        moved=4 * all_pairs * width,
    )

    reg_row = reg_step.reshape(1, row_count)
    dam_row = dam_step.reshape(1, dam_count)
    outgoing, place, history, reg_column = pack(routes.T, history, reg_row)
    for round_index in range(ROUNDS):
        received = exchange(outgoing, devices, capacity)
        back_start, ordered, columns, dam_force = dam_part(
            conn_free, conn_dam, dam_field, stiff_ref, stiff_coef, mass_coef
        )
        free_force, back = free_part(
            columns, received, ordered, stiff_coef, mass_coef, back_start
        )
        returned = exchange(back, devices, capacity)
        (dam_field,) = dam_update(conn_dam, free_force, dam_force, dam_field, dam_row)
        if round_index < ROUNDS - 1:
            history, outgoing = turn(place, returned, history, reg_column, dam_field)
        else:
            history, pulled = last(place, returned, history, reg_column, dam_field)
    return (history, pulled, dam_field)


def solution(mesh):
    rows = P(("reg", "dam"), None)
    flat = P(("reg", "dam"))
    in_specs = (rows, rows, rows, rows, rows, P(), flat, flat, flat, flat)
    return jax.shard_map(
        shards, mesh=mesh, in_specs=in_specs, out_specs=(rows, rows, rows), check_vma=False
    )
```

```python
import functools

import jax
import jax.numpy as jnp
from jax import lax
from jax.experimental import pallas as pl
from jax.experimental.pallas import tpu as pltpu
from jax.sharding import Mesh
from jax.sharding import PartitionSpec as P

ROUNDS = 2
AXES = ("reg_high", "dam", "reg_low")
GROUP = 8
VMEM_BYTES = 28 * 1024 * 1024
BF16 = jnp.bfloat16
F32 = jnp.float32


def mask_to_bf16(mask):
    return jnp.where(mask, 1.0, 0.0).astype(BF16)


def dot(left, right):
    return jnp.dot(left, right, preferred_element_type=F32)


def dot_first(left, right):
    return lax.dot_general(left, right, (((0,), (0,)), ((), ())), preferred_element_type=F32)


def transfer(pairs, sems):
    copies = [pltpu.make_async_copy(a, b, sems.at[i]) for i, (a, b) in enumerate(pairs)]
    for copy in copies:
        copy.start()
    return copies


def finish(copies):
    for copy in copies:
        copy.wait()


def as_column(row):
    size = row.shape[1]
    down = lax.broadcasted_iota(jnp.int32, (size, size), 0)
    across = lax.broadcasted_iota(jnp.int32, (size, size), 1)
    return jnp.sum(jnp.where(down == across, row, jnp.zeros_like(row)), axis=1, keepdims=True)


def block_of(device, dam):
    high = device // (2 * dam)
    rest = device - high * (2 * dam)
    low = rest // dam
    return (high * dam + rest - low * dam) * 2 + low


def pack_kernel(
    capacity,
    dam,
    routes_hbm,
    history_hbm,
    step_hbm,
    out_hbm,
    place_ref,
    history_ref,
    column_ref,
    routes_ref,
    step_ref,
    out_ref,
    sems,
):
    inward = transfer(
        [(routes_hbm, routes_ref), (history_hbm, history_ref), (step_hbm, step_ref)], sems
    )
    slots, rows = place_ref.shape
    finish(inward[:1])
    row0, row1 = routes_ref[0:1, :], routes_ref[1:2, :]
    col0, col1 = as_column(row0), as_column(row1)
    down = lax.broadcasted_iota(jnp.int32, (rows, rows), 0)
    across = lax.broadcasted_iota(jnp.int32, (rows, rows), 1)
    numbers = lax.broadcasted_iota(jnp.int32, (slots, rows), 0)
    hits = []
    for own in (row0, row1):
        same = jnp.where(col0 == own, 1, 0) + jnp.where(col1 == own, 1, 0)
        slot = jnp.sum(jnp.where(down < across, same, 0), axis=0, keepdims=True)
        hits.append(block_of(own, dam) * capacity + slot == numbers)
    place = mask_to_bf16(hits[0] | hits[1])
    place_ref[...] = place
    finish(inward[1:])
    out_ref[...] = dot(place, history_ref[...]).astype(BF16)
    outward = transfer([(out_ref, out_hbm)], sems)
    column_ref[...] = jnp.broadcast_to(as_column(step_ref[...]), column_ref.shape)
    finish(outward)


def turn_kernel(
    place_ref, returned_ref, history_ref, column_ref, after_hbm, next_ref, out_hbm, out_ref, sems
):
    place = place_ref[...]
    pulled = dot_first(place, returned_ref[...])
    following = (history_ref[...].astype(F32) - column_ref[:, 0:1] * pulled).astype(BF16)
    next_ref[...] = following
    out_ref[...] = dot(place, following).astype(BF16)
    finish(transfer([(out_ref, out_hbm)], sems))


def last_kernel(
    place_ref,
    returned_ref,
    history_ref,
    column_ref,
    after_hbm,
    next_hbm,
    pulled_hbm,
    next_ref,
    pulled_ref,
    sems,
):
    pulled = dot_first(place_ref[...], returned_ref[...])
    pulled_ref[...] = pulled
    outward = transfer([(pulled_ref, pulled_hbm)], sems)
    next_ref[...] = (history_ref[...].astype(F32) - column_ref[:, 0:1] * pulled).astype(BF16)
    finish(outward + transfer([(next_ref, next_hbm)], sems.at[1:2]))


def by_component(stiff):
    size = stiff.shape[0]
    nodes = size // 3
    down = lax.broadcasted_iota(jnp.int32, (size, size), 0)
    across = lax.broadcasted_iota(jnp.int32, (size, size), 1)
    part = (down >= nodes).astype(jnp.int32) + (down >= 2 * nodes).astype(jnp.int32)
    order = mask_to_bf16(across == 3 * (down - part * nodes) + part)
    half = dot(order, stiff).astype(BF16)
    return lax.dot_general(
        half, order, (((1,), (1,)), ((), ())), preferred_element_type=F32
    ).astype(BF16)


def select_rows(columns, first, width):
    nodes = columns.shape[0]
    lanes = lax.broadcasted_iota(jnp.int32, (nodes, width), 1).astype(jnp.int16)
    parts = []
    for e in range(first, first + GROUP):
        own = jnp.broadcast_to(columns[:, e : e + 1], (nodes, width)).astype(jnp.int16)
        parts.append(jnp.where(own == lanes, jnp.ones((), BF16), jnp.zeros((), BF16)))
    return jnp.concatenate(parts, axis=0)


def element_forces(u, stiff, stiff_coef_ref, mass_coef_ref, first):
    nodes = u.shape[0] // GROUP
    samples = u.shape[1] // 3
    lane = lax.broadcasted_iota(jnp.int32, (nodes, samples), 1).astype(jnp.int16)
    nothing = jnp.zeros((), BF16)

    def part(e, c):
        return u[e * nodes : (e + 1) * nodes, c * samples : (c + 1) * samples]

    blocks = []
    for pair in range(0, GROUP, 2):
        sides = [jnp.concatenate([part(e, c) for c in range(3)], axis=0) for e in (pair, pair + 1)]
        product = dot(stiff, jnp.concatenate(sides, axis=1))
        for side, e in enumerate((pair, pair + 1)):
            k = stiff_coef_ref[first + e]
            m = mass_coef_ref[first + e]
            row = []
            for c in range(3):
                own = product[c * nodes : (c + 1) * nodes, side * samples : (side + 1) * samples]
                w = part(e, c)
                before = jnp.where(lane == 0, nothing, pltpu.roll(w, 1, 1))
                after = jnp.where(lane == samples - 1, nothing, pltpu.roll(w, samples - 1, 1))
                accel = ((before + after) - (w + w)).astype(F32)
                row.append((k * own + m * accel).astype(BF16))
            blocks.append(jnp.concatenate(row, axis=1))
    return jnp.concatenate(blocks, axis=0)


def chunks_of(ref, groups):
    rows = ref.shape[0] // groups
    return [ref.at[g * rows : (g + 1) * rows, :] for g in range(groups)]


def sweep(groups, gather, forces, add):
    for turn in range(groups + 2):
        if turn >= 2:
            add(turn - 2)
        if 1 <= turn <= groups:
            forces(turn - 1)
        if turn < groups:
            gather(turn)


def forces_stage(held, stiff_ref, coefs, force_chunks):
    def stage(group):
        force_chunks[group][...] = element_forces(
            held[group % 2][...], stiff_ref[...], *coefs, group * GROUP
        )

    return stage


class Sender:
    def __init__(self, source, target, sems):
        self.chunks = chunks_of(source, sems.shape[0])
        self.targets = chunks_of(target, sems.shape[0])
        self.sems = sems
        self.started = []

    def start(self, group):
        copy = pltpu.make_async_copy(self.chunks[group], self.targets[group], self.sems.at[group])
        copy.start()
        self.started.append(copy)

    def finish(self):
        finish(self.started)


def dam_part_kernel(
    capacity,
    dam,
    free_hbm,
    dam_conn_hbm,
    dam_hbm,
    stiff_hbm,
    stiff_coef_hbm,
    mass_coef_hbm,
    back_hbm,
    order_ref,
    columns_ref,
    force_hbm,
    free_ref,
    dam_conn_ref,
    dam_ref,
    stiff_ref,
    stiff_coef_ref,
    mass_coef_ref,
    back_ref,
    force_ref,
    held0,
    held1,
    sems,
    force_sems,
):
    inward = transfer(
        [
            (dam_conn_hbm, dam_conn_ref),
            (dam_hbm, dam_ref),
            (stiff_hbm, stiff_ref),
            (free_hbm, free_ref),
            (stiff_coef_hbm, stiff_coef_ref),
            (mass_coef_hbm, mass_coef_ref),
        ],
        sems,
    )
    finish(inward)
    order_ref[...] = by_component(stiff_ref[...])
    dam_columns = dam_conn_ref[...].T
    free_columns = free_ref[...].T
    sender_of = free_columns // capacity
    free_columns = free_columns + (block_of(sender_of, dam) - sender_of) * capacity
    columns_ref[...] = free_columns
    groups = force_sems.shape[0]
    held = (held0, held1)
    sender = Sender(force_ref, force_hbm, force_sems)

    def gather(group):
        select = select_rows(dam_columns, group * GROUP, dam_ref.shape[0])
        held[group % 2][...] = dot(select, dam_ref[...]).astype(BF16)

    def add(group):
        sender.start(group)
        select = select_rows(free_columns, group * GROUP, back_ref.shape[1])
        part = dot_first(sender.chunks[group][...], select)
        back_ref[...] = part if group == 0 else back_ref[...] + part

    coefs = (stiff_coef_ref, mass_coef_ref)
    sweep(groups, gather, forces_stage(held, order_ref, coefs, sender.chunks), add)
    finish(transfer([(back_ref, back_hbm)], sems))
    sender.finish()


def free_part_kernel(
    columns_ref,
    received_ref,
    order_ref,
    stiff_coef_hbm,
    mass_coef_hbm,
    start_hbm,
    force_hbm,
    back_hbm,
    stiff_coef_ref,
    mass_coef_ref,
    start_ref,
    total_ref,
    made,
    force_ref,
    back_ref,
    held0,
    held1,
    sems,
    force_sems,
):
    inward = transfer(
        [
            (stiff_coef_hbm, stiff_coef_ref),
            (mass_coef_hbm, mass_coef_ref),
            (start_hbm, start_ref),
        ],
        sems,
    )
    columns = columns_ref[...]
    groups = force_sems.shape[0]
    made_chunks = chunks_of(made, groups)
    held = (held0, held1)
    sender = Sender(force_ref, force_hbm, force_sems)

    def gather(group):
        select = select_rows(columns, group * GROUP, received_ref.shape[0])
        made_chunks[group][...] = select
        held[group % 2][...] = dot(select, received_ref[...]).astype(BF16)
        if group == 0:
            finish(inward[:2])

    def add(group):
        sender.start(group)
        part = dot_first(sender.chunks[group][...], made_chunks[group][...])
        total_ref[...] = part if group == 0 else total_ref[...] + part

    coefs = (stiff_coef_ref, mass_coef_ref)
    sweep(groups, gather, forces_stage(held, order_ref, coefs, sender.chunks), add)
    finish(inward[2:])
    slots = total_ref.shape[1]
    quarter = slots // 4
    outward = []
    for i in range(4):
        rows = slice(i * quarter, (i + 1) * quarter)
        back_ref[rows, :] = (start_ref[:, rows] + total_ref[:, rows]).T.astype(BF16)
        copy = pltpu.make_async_copy(back_ref.at[rows, :], back_hbm.at[rows, :], sems.at[i])
        copy.start()
        outward.append(copy)
    finish(outward)
    sender.finish()


def dam_update_kernel(
    dam_conn_hbm,
    free_force_hbm,
    dam_force_hbm,
    dam_hbm,
    step_hbm,
    next_hbm,
    dam_conn_ref,
    free_force,
    dam_force,
    total_ref,
    dam_ref,
    step_ref,
    next_ref,
    sems,
    free_sems,
    dam_sems,
):
    groups = free_sems.shape[0]
    inward = transfer([(dam_conn_hbm, dam_conn_ref), (dam_hbm, dam_ref), (step_hbm, step_ref)], sems)
    free_chunks, dam_chunks = chunks_of(free_force, groups), chunks_of(dam_force, groups)
    free_copies = transfer(list(zip(chunks_of(free_force_hbm, groups), free_chunks)), free_sems)
    dam_copies = transfer(list(zip(chunks_of(dam_force_hbm, groups), dam_chunks)), dam_sems)
    finish(inward)
    columns = dam_conn_ref[...].T
    for group in range(groups):
        finish([free_copies[group], dam_copies[group]])
        force = free_chunks[group][...].astype(F32) + dam_chunks[group][...].astype(F32)
        select = select_rows(columns, group * GROUP, dam_ref.shape[0])
        part = dot_first(force.astype(BF16), select)
        total_ref[...] = part if group == 0 else total_ref[...] + part
    step = as_column(step_ref[...])
    next_ref[...] = (dam_ref[...].astype(F32) - step * total_ref[...].T).astype(BF16)
    finish(transfer([(next_ref, next_hbm)], sems))


def exchange(rows, devices, capacity):
    width = rows.shape[1]
    shaped = rows.reshape(devices, capacity, width)
    arrived = lax.all_to_all(shaped, AXES, split_axis=0, concat_axis=0, tiled=True)
    return arrived.reshape(devices * capacity, width)


def kernel(body, name, ins, outs, scratch, flops=0, moved=0):
    hbm = pl.BlockSpec(memory_space=pltpu.HBM)
    vmem = pl.BlockSpec(memory_space=pltpu.VMEM)
    spaces = {"h": pltpu.HBM, "v": pltpu.VMEM}
    call = pl.pallas_call(
        body,
        name=name,
        in_specs=[hbm if letter == "h" else vmem for letter in ins],
        out_specs=[hbm if out[0] == "h" else vmem for out in outs],
        out_shape=[spaces[out[0]](*out[1:]) for out in outs],
        scratch_shapes=scratch,
        compiler_params=pltpu.CompilerParams(vmem_limit_bytes=VMEM_BYTES),
        cost_estimate=pl.CostEstimate(flops=flops, bytes_accessed=moved, transcendentals=0),
    )

    def run(*operands):
        return call(
            *[
                x if letter == "a" else pltpu.with_memory_space_constraint(x, spaces[letter])
                for letter, x in zip(ins, operands)
            ]
        )

    return run


def shards(
    history,
    routes,
    dam_field,
    conn_free,
    conn_dam,
    stiff_ref,
    stiff_coef,
    mass_coef,
    reg_step,
    dam_step,
):
    devices = lax.axis_size(AXES)
    row_count, width = history.shape
    capacity = 4 * row_count // devices
    slots = devices * capacity
    dam_count = dam_field.shape[0]
    elements, nodes = conn_free.shape
    all_pairs = elements * nodes
    pairs = GROUP * nodes
    groups = elements // GROUP

    I32 = jnp.int32
    vmem = pltpu.VMEM
    dma = pltpu.SemaphoreType.DMA
    conn = vmem((elements, nodes), I32)
    stiff = vmem(stiff_ref.shape, BF16)
    coefs = [pltpu.SMEM((elements,), F32)] * 2
    held = [vmem((pairs, width), BF16)] * 2
    forces_type = ((all_pairs, width), BF16)
    free_type = ((all_pairs, slots), BF16)
    back_type = ((width, slots), F32)
    stiff_type = (stiff_ref.shape, BF16)
    place_type = ((slots, row_count), BF16)
    slots_type = ((slots, width), BF16)
    rows_type = ((row_count, width), BF16)
    pulled_type = ((row_count, width), F32)
    column_type = ((row_count, 128), F32)
    dam_type = ((dam_count, width), BF16)
    product = 2 * all_pairs * slots * width

    pack = kernel(
        functools.partial(pack_kernel, capacity, lax.axis_size("dam")),
        "pack",
        "hhh",
        [("h", *slots_type), ("v", *place_type), ("v", *rows_type), ("v", *column_type)],
        [vmem((2, row_count), I32), vmem((1, row_count), F32), vmem(*slots_type), dma((3,))],
    )
    turn = kernel(
        turn_kernel,
        "turn",
        "vavvh",
        [("v", *rows_type), ("h", *slots_type)],
        [vmem(*slots_type), dma((1,))],
    )
    last = kernel(
        last_kernel,
        "last",
        "vavvh",
        [("h", *rows_type), ("h", *pulled_type)],
        [vmem(*rows_type), vmem(*pulled_type), dma((2,))],
    )
    dam_part = kernel(
        functools.partial(dam_part_kernel, capacity, lax.axis_size("dam")),
        "dam_part",
        "hhhhhh",
        [("h", *back_type), ("v", *stiff_type), ("v", (nodes, elements), I32), ("h", *forces_type)],
        [conn, conn, vmem(*dam_type), stiff, *coefs, vmem(*back_type), vmem(*forces_type)]
        + [*held, dma((6,)), dma((groups,))],
        flops=3 * product,
        moved=4 * all_pairs * width,
    )
    free_part = kernel(
        free_part_kernel,
        "free_part",
        "vavhhh",
        [("h", *forces_type), ("h", *slots_type)],
        [*coefs, vmem(*back_type), vmem(*back_type)]
        + [vmem(*free_type), vmem(*forces_type), vmem(*slots_type), *held]
        + [dma((4,)), dma((groups,))],
        flops=3 * product,
        moved=4 * all_pairs * width,
    )
    dam_update = kernel(
        dam_update_kernel,
        "dam_update",
        "hhhhh",
        [("h", *dam_type)],
        [conn, vmem(*forces_type), vmem(*forces_type)]
        + [vmem((width, dam_count), F32), vmem(*dam_type), vmem((1, dam_count), F32)]
        + [vmem(*dam_type), dma((3,)), dma((groups,)), dma((groups,))],
        flops=product,
        moved=4 * all_pairs * width,
    )

    reg_row = reg_step.reshape(1, row_count)
    dam_row = dam_step.reshape(1, dam_count)
    outgoing, place, history, reg_column = pack(routes.T, history, reg_row)
    for round_index in range(ROUNDS):
        received = exchange(outgoing, devices, capacity)
        back_start, ordered, columns, dam_force = dam_part(
            conn_free, conn_dam, dam_field, stiff_ref, stiff_coef, mass_coef
        )
        free_force, back = free_part(
            columns, received, ordered, stiff_coef, mass_coef, back_start
        )
        returned = exchange(back, devices, capacity)
        (dam_field,) = dam_update(conn_dam, free_force, dam_force, dam_field, dam_row)
        if round_index < ROUNDS - 1:
            history, outgoing = turn(place, returned, history, reg_column, dam_field)
        else:
            history, pulled = last(place, returned, history, reg_column, dam_field)
    return (history, pulled, dam_field)


def solution(mesh):
    reg, dam = mesh.devices.shape
    split = Mesh(mesh.devices.reshape(reg // 2, 2, dam), ("reg_high", "reg_low", "dam"))
    axes = ("reg_high", "reg_low", "dam")
    rows = P(axes, None)
    flat = P(axes)
    in_specs = (rows, rows, rows, rows, rows, P(), flat, flat, flat, flat)
    return jax.shard_map(
        shards, mesh=split, in_specs=in_specs, out_specs=(rows, rows, rows), check_vma=False
    )
```

```python
import functools

import jax
import jax.numpy as jnp
from jax import lax
from jax.experimental import pallas as pl
from jax.experimental.pallas import tpu as pltpu
from jax.sharding import Mesh
from jax.sharding import PartitionSpec as P

ROUNDS = 2
AXES = ("reg_high", "dam", "reg_low")
GROUP = 16
LANES = 128
VMEM_BYTES = 28 * 1024 * 1024
BF16 = jnp.bfloat16
F32 = jnp.float32


def mask_to_bf16(mask):
    return jnp.where(mask, 1.0, 0.0).astype(BF16)


def dot(left, right):
    return jnp.dot(left, right, preferred_element_type=F32)


def dot_first(left, right):
    return lax.dot_general(left, right, (((0,), (0,)), ((), ())), preferred_element_type=F32)


def transfer(pairs, sems):
    copies = [pltpu.make_async_copy(a, b, sems.at[i]) for i, (a, b) in enumerate(pairs)]
    for copy in copies:
        copy.start()
    return copies


def finish(copies):
    for copy in copies:
        copy.wait()


def as_column(row):
    size = row.shape[1]
    down = lax.broadcasted_iota(jnp.int32, (size, size), 0)
    across = lax.broadcasted_iota(jnp.int32, (size, size), 1)
    return jnp.sum(jnp.where(down == across, row, jnp.zeros_like(row)), axis=1, keepdims=True)


def block_of(device, dam):
    high = device // (2 * dam)
    rest = device - high * (2 * dam)
    low = rest // dam
    return (high * dam + rest - low * dam) * 2 + low


def pack_kernel(
    capacity,
    dam,
    routes_hbm,
    history_hbm,
    step_hbm,
    out_hbm,
    place_ref,
    history_ref,
    column_ref,
    routes_ref,
    step_ref,
    out_ref,
    sems,
):
    inward = transfer(
        [(routes_hbm, routes_ref), (history_hbm, history_ref), (step_hbm, step_ref)], sems
    )
    slots, rows = place_ref.shape
    finish(inward[:1])
    row0, row1 = routes_ref[0:1, :], routes_ref[1:2, :]
    col0, col1 = as_column(row0), as_column(row1)
    down = lax.broadcasted_iota(jnp.int32, (rows, rows), 0)
    across = lax.broadcasted_iota(jnp.int32, (rows, rows), 1)
    numbers = lax.broadcasted_iota(jnp.int32, (slots, rows), 0)
    hits = []
    for own in (row0, row1):
        same = jnp.where(col0 == own, 1, 0) + jnp.where(col1 == own, 1, 0)
        slot = jnp.sum(jnp.where(down < across, same, 0), axis=0, keepdims=True)
        hits.append(block_of(own, dam) * capacity + slot == numbers)
    place = mask_to_bf16(hits[0] | hits[1])
    place_ref[...] = place
    finish(inward[1:])
    out_ref[...] = dot(place, history_ref[...]).astype(BF16)
    outward = transfer([(out_ref, out_hbm)], sems)
    column_ref[...] = jnp.broadcast_to(as_column(step_ref[...]), column_ref.shape)
    finish(outward)


def turn_kernel(
    place_ref, returned_ref, history_ref, column_ref, after_hbm, next_ref, out_hbm, out_ref, sems
):
    place = place_ref[...]
    pulled = dot_first(place, returned_ref[...])
    following = (history_ref[...].astype(F32) - column_ref[:, 0:1] * pulled).astype(BF16)
    next_ref[...] = following
    out_ref[...] = dot(place, following).astype(BF16)
    finish(transfer([(out_ref, out_hbm)], sems))


def last_kernel(
    place_ref,
    returned_ref,
    history_ref,
    column_ref,
    after_hbm,
    next_hbm,
    pulled_hbm,
    next_ref,
    pulled_ref,
    sems,
):
    pulled = dot_first(place_ref[...], returned_ref[...])
    pulled_ref[...] = pulled
    outward = transfer([(pulled_ref, pulled_hbm)], sems)
    next_ref[...] = (history_ref[...].astype(F32) - column_ref[:, 0:1] * pulled).astype(BF16)
    finish(outward + transfer([(next_ref, next_hbm)], sems.at[1:2]))


def by_component(stiff):
    size = stiff.shape[0]
    nodes = size // 3
    down = lax.broadcasted_iota(jnp.int32, (size, size), 0)
    across = lax.broadcasted_iota(jnp.int32, (size, size), 1)
    part = (down >= nodes).astype(jnp.int32) + (down >= 2 * nodes).astype(jnp.int32)
    order = mask_to_bf16(across == 3 * (down - part * nodes) + part)
    half = dot(order, stiff).astype(BF16)
    return lax.dot_general(
        half, order, (((1,), (1,)), ((), ())), preferred_element_type=F32
    ).astype(BF16)


def select_rows(columns, first, width):
    nodes = columns.shape[0]
    lanes = lax.broadcasted_iota(jnp.int32, (nodes, width), 1).astype(jnp.int16)
    parts = []
    for e in range(first, first + GROUP):
        own = jnp.broadcast_to(columns[:, e : e + 1], (nodes, LANES)).astype(jnp.int16)
        own = jnp.concatenate([own] * (width // LANES), axis=1)
        parts.append(jnp.where(own == lanes, jnp.ones((), BF16), jnp.zeros((), BF16)))
    return jnp.concatenate(parts, axis=0)


def select_spread(spread, width):
    own = jnp.concatenate([spread] * (width // LANES), axis=1)
    lanes = lax.broadcasted_iota(jnp.int32, own.shape, 1).astype(jnp.int16)
    return jnp.where(own == lanes, jnp.ones((), BF16), jnp.zeros((), BF16))


def element_forces(u, stiff, stiff_coef_ref, mass_coef_ref, first):
    nodes = u.shape[0] // GROUP
    samples = u.shape[1] // 3
    lane = lax.broadcasted_iota(jnp.int32, (nodes, samples), 1).astype(jnp.int16)
    nothing = jnp.zeros((), BF16)

    def part(e, c):
        return u[e * nodes : (e + 1) * nodes, c * samples : (c + 1) * samples]

    blocks = []
    for pair in range(0, GROUP, 2):
        sides = [jnp.concatenate([part(e, c) for c in range(3)], axis=0) for e in (pair, pair + 1)]
        product = dot(stiff, jnp.concatenate(sides, axis=1))
        for side, e in enumerate((pair, pair + 1)):
            k = stiff_coef_ref[first + e]
            m = mass_coef_ref[first + e]
            row = []
            for c in range(3):
                own = product[c * nodes : (c + 1) * nodes, side * samples : (side + 1) * samples]
                w = part(e, c)
                before = jnp.where(lane == 0, nothing, pltpu.roll(w, 1, 1))
                after = jnp.where(lane == samples - 1, nothing, pltpu.roll(w, samples - 1, 1))
                accel = ((before + after) - (w + w)).astype(F32)
                row.append((k * own + m * accel).astype(BF16))
            blocks.append(jnp.concatenate(row, axis=1))
    return jnp.concatenate(blocks, axis=0)


def chunks_of(ref, groups):
    rows = ref.shape[0] // groups
    return [ref.at[g * rows : (g + 1) * rows, :] for g in range(groups)]


def sweep(groups, gather, forces, add):
    for turn in range(groups + 2):
        if turn >= 2:
            add(turn - 2)
        if 1 <= turn <= groups:
            forces(turn - 1)
        if turn < groups:
            gather(turn)


def forces_stage(held, stiff_ref, coefs, force_chunks):
    def stage(group):
        force_chunks[group][...] = element_forces(
            held[group % 2][...], stiff_ref[...], *coefs, group * GROUP
        )

    return stage


class Sender:
    def __init__(self, source, target, sems):
        self.chunks = chunks_of(source, sems.shape[0])
        self.targets = chunks_of(target, sems.shape[0])
        self.sems = sems
        self.started = []

    def start(self, group):
        copy = pltpu.make_async_copy(self.chunks[group], self.targets[group], self.sems.at[group])
        copy.start()
        self.started.append(copy)

    def finish(self):
        finish(self.started)


def dam_part_kernel(
    capacity,
    dam,
    free_hbm,
    dam_conn_hbm,
    dam_hbm,
    stiff_hbm,
    stiff_coef_hbm,
    mass_coef_hbm,
    back_hbm,
    order_ref,
    columns_ref,
    force_hbm,
    free_ref,
    dam_conn_ref,
    dam_ref,
    stiff_ref,
    stiff_coef_ref,
    mass_coef_ref,
    back_ref,
    force_ref,
    held0,
    held1,
    sems,
    force_sems,
):
    inward = transfer(
        [
            (dam_conn_hbm, dam_conn_ref),
            (dam_hbm, dam_ref),
            (stiff_hbm, stiff_ref),
            (free_hbm, free_ref),
            (stiff_coef_hbm, stiff_coef_ref),
            (mass_coef_hbm, mass_coef_ref),
        ],
        sems,
    )
    finish(inward)
    order_ref[...] = by_component(stiff_ref[...])
    dam_columns = dam_conn_ref[...].T
    free_columns = free_ref[...].T
    sender_of = free_columns // capacity
    free_columns = free_columns + (block_of(sender_of, dam) - sender_of) * capacity
    nodes = free_columns.shape[0]
    for e in range(free_columns.shape[1]):
        own = jnp.broadcast_to(free_columns[:, e : e + 1], (nodes, LANES))
        columns_ref[e * nodes : (e + 1) * nodes, :] = own.astype(jnp.int16)
    groups = force_sems.shape[0]
    held = (held0, held1)
    sender = Sender(force_ref, force_hbm, force_sems)

    def gather(group):
        select = select_rows(dam_columns, group * GROUP, dam_ref.shape[0])
        held[group % 2][...] = dot(select, dam_ref[...]).astype(BF16)

    def add(group):
        sender.start(group)
        select = select_spread(chunks_of(columns_ref, groups)[group][...], back_ref.shape[1])
        part = dot_first(sender.chunks[group][...], select)
        back_ref[...] = part if group == 0 else back_ref[...] + part

    coefs = (stiff_coef_ref, mass_coef_ref)
    sweep(groups, gather, forces_stage(held, order_ref, coefs, sender.chunks), add)
    finish(transfer([(back_ref, back_hbm)], sems))
    sender.finish()


def free_part_kernel(
    columns_ref,
    received_ref,
    order_ref,
    stiff_coef_hbm,
    mass_coef_hbm,
    start_hbm,
    force_hbm,
    back_hbm,
    stiff_coef_ref,
    mass_coef_ref,
    start_ref,
    total_ref,
    made,
    force_ref,
    back_ref,
    held0,
    held1,
    sems,
    force_sems,
):
    inward = transfer(
        [
            (stiff_coef_hbm, stiff_coef_ref),
            (mass_coef_hbm, mass_coef_ref),
            (start_hbm, start_ref),
        ],
        sems,
    )
    groups = force_sems.shape[0]
    made_chunks = chunks_of(made, groups)
    held = (held0, held1)
    sender = Sender(force_ref, force_hbm, force_sems)

    def gather(group):
        select = select_spread(chunks_of(columns_ref, groups)[group][...], received_ref.shape[0])
        made_chunks[group][...] = select
        held[group % 2][...] = dot(select, received_ref[...]).astype(BF16)
        if group == 0:
            finish(inward[:2])

    def add(group):
        sender.start(group)
        part = dot_first(sender.chunks[group][...], made_chunks[group][...])
        total_ref[...] = part if group == 0 else total_ref[...] + part

    coefs = (stiff_coef_ref, mass_coef_ref)
    sweep(groups, gather, forces_stage(held, order_ref, coefs, sender.chunks), add)
    finish(inward[2:])
    slots = total_ref.shape[1]
    quarter = slots // 4
    outward = []
    for i in range(4):
        rows = slice(i * quarter, (i + 1) * quarter)
        back_ref[rows, :] = (start_ref[:, rows] + total_ref[:, rows]).T.astype(BF16)
        copy = pltpu.make_async_copy(back_ref.at[rows, :], back_hbm.at[rows, :], sems.at[i])
        copy.start()
        outward.append(copy)
    finish(outward)
    sender.finish()


def dam_update_kernel(
    dam_conn_hbm,
    free_force_hbm,
    dam_force_hbm,
    dam_hbm,
    step_hbm,
    next_hbm,
    dam_conn_ref,
    free_force,
    dam_force,
    total_ref,
    dam_ref,
    step_ref,
    next_ref,
    sems,
    free_sems,
    dam_sems,
):
    groups = free_sems.shape[0]
    inward = transfer([(dam_conn_hbm, dam_conn_ref), (dam_hbm, dam_ref), (step_hbm, step_ref)], sems)
    free_chunks, dam_chunks = chunks_of(free_force, groups), chunks_of(dam_force, groups)
    free_copies = transfer(list(zip(chunks_of(free_force_hbm, groups), free_chunks)), free_sems)
    dam_copies = transfer(list(zip(chunks_of(dam_force_hbm, groups), dam_chunks)), dam_sems)
    finish(inward)
    columns = dam_conn_ref[...].T
    for group in range(groups):
        finish([free_copies[group], dam_copies[group]])
        force = free_chunks[group][...].astype(F32) + dam_chunks[group][...].astype(F32)
        select = select_rows(columns, group * GROUP, dam_ref.shape[0])
        part = dot_first(force.astype(BF16), select)
        total_ref[...] = part if group == 0 else total_ref[...] + part
    step = as_column(step_ref[...])
    next_ref[...] = (dam_ref[...].astype(F32) - step * total_ref[...].T).astype(BF16)
    finish(transfer([(next_ref, next_hbm)], sems))


def exchange(rows, devices, capacity):
    width = rows.shape[1]
    shaped = rows.reshape(devices, capacity, width)
    arrived = lax.all_to_all(shaped, AXES, split_axis=0, concat_axis=0, tiled=True)
    return arrived.reshape(devices * capacity, width)


def kernel(body, name, ins, outs, scratch, flops=0, moved=0):
    hbm = pl.BlockSpec(memory_space=pltpu.HBM)
    vmem = pl.BlockSpec(memory_space=pltpu.VMEM)
    spaces = {"h": pltpu.HBM, "v": pltpu.VMEM}
    call = pl.pallas_call(
        body,
        name=name,
        in_specs=[hbm if letter == "h" else vmem for letter in ins],
        out_specs=[hbm if out[0] == "h" else vmem for out in outs],
        out_shape=[spaces[out[0]](*out[1:]) for out in outs],
        scratch_shapes=scratch,
        compiler_params=pltpu.CompilerParams(vmem_limit_bytes=VMEM_BYTES),
        cost_estimate=pl.CostEstimate(flops=flops, bytes_accessed=moved, transcendentals=0),
    )

    def run(*operands):
        return call(
            *[
                x if letter == "a" else pltpu.with_memory_space_constraint(x, spaces[letter])
                for letter, x in zip(ins, operands)
            ]
        )

    return run


def shards(
    history,
    routes,
    dam_field,
    conn_free,
    conn_dam,
    stiff_ref,
    stiff_coef,
    mass_coef,
    reg_step,
    dam_step,
):
    devices = lax.axis_size(AXES)
    row_count, width = history.shape
    capacity = 4 * row_count // devices
    slots = devices * capacity
    dam_count = dam_field.shape[0]
    elements, nodes = conn_free.shape
    all_pairs = elements * nodes
    pairs = GROUP * nodes
    groups = elements // GROUP

    I32 = jnp.int32
    vmem = pltpu.VMEM
    dma = pltpu.SemaphoreType.DMA
    conn = vmem((elements, nodes), I32)
    stiff = vmem(stiff_ref.shape, BF16)
    coefs = [pltpu.SMEM((elements,), F32)] * 2
    held = [vmem((pairs, width), BF16)] * 2
    forces_type = ((all_pairs, width), BF16)
    free_type = ((all_pairs, slots), BF16)
    back_type = ((width, slots), F32)
    stiff_type = (stiff_ref.shape, BF16)
    place_type = ((slots, row_count), BF16)
    slots_type = ((slots, width), BF16)
    rows_type = ((row_count, width), BF16)
    pulled_type = ((row_count, width), F32)
    column_type = ((row_count, 128), F32)
    dam_type = ((dam_count, width), BF16)
    product = 2 * all_pairs * slots * width

    pack = kernel(
        functools.partial(pack_kernel, capacity, lax.axis_size("dam")),
        "pack",
        "hhh",
        [("h", *slots_type), ("v", *place_type), ("v", *rows_type), ("v", *column_type)],
        [vmem((2, row_count), I32), vmem((1, row_count), F32), vmem(*slots_type), dma((3,))],
    )
    turn = kernel(
        turn_kernel,
        "turn",
        "vavvh",
        [("v", *rows_type), ("h", *slots_type)],
        [vmem(*slots_type), dma((1,))],
    )
    last = kernel(
        last_kernel,
        "last",
        "vavvh",
        [("h", *rows_type), ("h", *pulled_type)],
        [vmem(*rows_type), vmem(*pulled_type), dma((2,))],
    )
    dam_part = kernel(
        functools.partial(dam_part_kernel, capacity, lax.axis_size("dam")),
        "dam_part",
        "hhhhhh",
        [("h", *back_type), ("v", *stiff_type), ("v", (all_pairs, LANES), jnp.int16), ("h", *forces_type)],
        [conn, conn, vmem(*dam_type), stiff, *coefs, vmem(*back_type), vmem(*forces_type)]
        + [*held, dma((6,)), dma((groups,))],
        flops=3 * product,
        moved=4 * all_pairs * width,
    )
    free_part = kernel(
        free_part_kernel,
        "free_part",
        "vavhhh",
        [("h", *forces_type), ("h", *slots_type)],
        [*coefs, vmem(*back_type), vmem(*back_type)]
        + [vmem(*free_type), vmem(*forces_type), vmem(*slots_type), *held]
        + [dma((4,)), dma((groups,))],
        flops=3 * product,
        moved=4 * all_pairs * width,
    )
    dam_update = kernel(
        dam_update_kernel,
        "dam_update",
        "hhhhh",
        [("h", *dam_type)],
        [conn, vmem(*forces_type), vmem(*forces_type)]
        + [vmem((width, dam_count), F32), vmem(*dam_type), vmem((1, dam_count), F32)]
        + [vmem(*dam_type), dma((3,)), dma((groups,)), dma((groups,))],
        flops=product,
        moved=4 * all_pairs * width,
    )

    reg_row = reg_step.reshape(1, row_count)
    dam_row = dam_step.reshape(1, dam_count)
    outgoing, place, history, reg_column = pack(routes.T, history, reg_row)
    for round_index in range(ROUNDS):
        received = exchange(outgoing, devices, capacity)
        back_start, ordered, columns, dam_force = dam_part(
            conn_free, conn_dam, dam_field, stiff_ref, stiff_coef, mass_coef
        )
        free_force, back = free_part(
            columns, received, ordered, stiff_coef, mass_coef, back_start
        )
        returned = exchange(back, devices, capacity)
        (dam_field,) = dam_update(conn_dam, free_force, dam_force, dam_field, dam_row)
        if round_index < ROUNDS - 1:
            history, outgoing = turn(place, returned, history, reg_column, dam_field)
        else:
            history, pulled = last(place, returned, history, reg_column, dam_field)
    return (history, pulled, dam_field)


def solution(mesh):
    reg, dam = mesh.devices.shape
    split = Mesh(mesh.devices.reshape(reg // 2, 2, dam), ("reg_high", "reg_low", "dam"))
    axes = ("reg_high", "reg_low", "dam")
    rows = P(axes, None)
    flat = P(axes)
    in_specs = (rows, rows, rows, rows, rows, P(), flat, flat, flat, flat)
    return jax.shard_map(
        shards, mesh=split, in_specs=in_specs, out_specs=(rows, rows, rows), check_vma=False
    )
```

```python
import functools

import jax
import jax.numpy as jnp
from jax import lax
from jax.experimental import pallas as pl
from jax.experimental.pallas import tpu as pltpu
from jax.sharding import Mesh
from jax.sharding import PartitionSpec as P

ROUNDS = 2
AXES = ("reg_high", "dam", "reg_low")
GROUP = 16
LANES = 128
VMEM_BYTES = 28 * 1024 * 1024
BF16 = jnp.bfloat16
F32 = jnp.float32


def mask_to_bf16(mask):
    return jnp.where(mask, 1.0, 0.0).astype(BF16)


def dot(left, right):
    return jnp.dot(left, right, preferred_element_type=F32)


def dot_first(left, right):
    return lax.dot_general(left, right, (((0,), (0,)), ((), ())), preferred_element_type=F32)


def transfer(pairs, sems):
    copies = [pltpu.make_async_copy(a, b, sems.at[i]) for i, (a, b) in enumerate(pairs)]
    for copy in copies:
        copy.start()
    return copies


def finish(copies):
    for copy in copies:
        copy.wait()


def as_column(row):
    size = row.shape[1]
    down = lax.broadcasted_iota(jnp.int32, (size, size), 0)
    across = lax.broadcasted_iota(jnp.int32, (size, size), 1)
    return jnp.sum(jnp.where(down == across, row, jnp.zeros_like(row)), axis=1, keepdims=True)


def block_of(device, dam):
    high = device // (2 * dam)
    rest = device - high * (2 * dam)
    low = rest // dam
    return (high * dam + rest - low * dam) * 2 + low


def pack_kernel(
    capacity,
    dam,
    routes_hbm,
    history_hbm,
    step_hbm,
    out_hbm,
    place_ref,
    history_ref,
    column_ref,
    routes_ref,
    step_ref,
    out_ref,
    sems,
):
    inward = transfer(
        [(routes_hbm, routes_ref), (history_hbm, history_ref), (step_hbm, step_ref)], sems
    )
    slots, rows = place_ref.shape
    finish(inward[:1])
    row0, row1 = routes_ref[0:1, :], routes_ref[1:2, :]
    col0, col1 = as_column(row0), as_column(row1)
    down = lax.broadcasted_iota(jnp.int32, (rows, rows), 0)
    across = lax.broadcasted_iota(jnp.int32, (rows, rows), 1)
    numbers = lax.broadcasted_iota(jnp.int32, (slots, rows), 0)
    hits = []
    for own in (row0, row1):
        same = jnp.where(col0 == own, 1, 0) + jnp.where(col1 == own, 1, 0)
        slot = jnp.sum(jnp.where(down < across, same, 0), axis=0, keepdims=True)
        hits.append(block_of(own, dam) * capacity + slot == numbers)
    place = mask_to_bf16(hits[0] | hits[1])
    place_ref[...] = place
    finish(inward[1:])
    out_ref[...] = dot(place, history_ref[...]).astype(BF16)
    outward = transfer([(out_ref, out_hbm)], sems)
    column_ref[...] = jnp.broadcast_to(as_column(step_ref[...]), column_ref.shape)
    finish(outward)


def turn_kernel(
    place_ref, returned_ref, history_ref, column_ref, after_hbm, next_ref, out_hbm, out_ref, sems
):
    place = place_ref[...]
    pulled = dot_first(place, returned_ref[...])
    following = (history_ref[...].astype(F32) - column_ref[:, 0:1] * pulled).astype(BF16)
    next_ref[...] = following
    out_ref[...] = dot(place, following).astype(BF16)
    finish(transfer([(out_ref, out_hbm)], sems))


def last_kernel(
    place_ref,
    returned_ref,
    history_ref,
    column_ref,
    after_hbm,
    next_hbm,
    pulled_hbm,
    next_ref,
    pulled_ref,
    sems,
):
    pulled = dot_first(place_ref[...], returned_ref[...])
    pulled_ref[...] = pulled
    outward = transfer([(pulled_ref, pulled_hbm)], sems)
    next_ref[...] = (history_ref[...].astype(F32) - column_ref[:, 0:1] * pulled).astype(BF16)
    finish(outward + transfer([(next_ref, next_hbm)], sems.at[1:2]))


def by_component(stiff):
    size = stiff.shape[0]
    nodes = size // 3
    down = lax.broadcasted_iota(jnp.int32, (size, size), 0)
    across = lax.broadcasted_iota(jnp.int32, (size, size), 1)
    part = (down >= nodes).astype(jnp.int32) + (down >= 2 * nodes).astype(jnp.int32)
    order = mask_to_bf16(across == 3 * (down - part * nodes) + part)
    half = dot(order, stiff).astype(BF16)
    return lax.dot_general(
        half, order, (((1,), (1,)), ((), ())), preferred_element_type=F32
    ).astype(BF16)


def select_rows(columns, first, width):
    nodes = columns.shape[0]
    lanes = lax.broadcasted_iota(jnp.int32, (nodes, width), 1).astype(jnp.int16)
    parts = []
    for e in range(first, first + GROUP):
        own = jnp.broadcast_to(columns[:, e : e + 1], (nodes, LANES)).astype(jnp.int16)
        own = jnp.concatenate([own] * (width // LANES), axis=1)
        parts.append(jnp.where(own == lanes, jnp.ones((), BF16), jnp.zeros((), BF16)))
    return jnp.concatenate(parts, axis=0)


def select_spread(spread, width):
    own = jnp.concatenate([spread] * (width // LANES), axis=1)
    lanes = lax.broadcasted_iota(jnp.int32, own.shape, 1).astype(jnp.int16)
    return jnp.where(own == lanes, jnp.ones((), BF16), jnp.zeros((), BF16))


def element_forces(u, stiff, stiff_coef_ref, mass_coef_ref, first):
    nodes = u.shape[0] // GROUP
    samples = u.shape[1] // 3
    lane = lax.broadcasted_iota(jnp.int32, (nodes, samples), 1).astype(jnp.int16)
    nothing = jnp.zeros((), BF16)

    def part(e, c):
        return u[e * nodes : (e + 1) * nodes, c * samples : (c + 1) * samples]

    blocks = []
    for pair in range(0, GROUP, 2):
        sides = [jnp.concatenate([part(e, c) for c in range(3)], axis=0) for e in (pair, pair + 1)]
        product = dot(stiff, jnp.concatenate(sides, axis=1))
        for side, e in enumerate((pair, pair + 1)):
            k = stiff_coef_ref[first + e]
            m = mass_coef_ref[first + e]
            row = []
            for c in range(3):
                own = product[c * nodes : (c + 1) * nodes, side * samples : (side + 1) * samples]
                w = part(e, c)
                before = jnp.where(lane == 0, nothing, pltpu.roll(w, 1, 1))
                after = jnp.where(lane == samples - 1, nothing, pltpu.roll(w, samples - 1, 1))
                accel = ((after - w) + (before - w)).astype(F32)
                row.append((k * own + m * accel).astype(BF16))
            blocks.append(jnp.concatenate(row, axis=1))
    return jnp.concatenate(blocks, axis=0)


def chunks_of(ref, groups):
    rows = ref.shape[0] // groups
    return [ref.at[g * rows : (g + 1) * rows, :] for g in range(groups)]


def sweep(groups, gather, forces, add):
    for turn in range(groups + 2):
        if turn >= 2:
            add(turn - 2)
        if 1 <= turn <= groups:
            forces(turn - 1)
        if turn < groups:
            gather(turn)


def forces_stage(held, stiff_ref, coefs, force_chunks):
    def stage(group):
        force_chunks[group][...] = element_forces(
            held[group % 2][...], stiff_ref[...], *coefs, group * GROUP
        )

    return stage


class Sender:
    def __init__(self, source, target, sems):
        self.chunks = chunks_of(source, sems.shape[0])
        self.targets = chunks_of(target, sems.shape[0])
        self.sems = sems
        self.started = []

    def start(self, group):
        copy = pltpu.make_async_copy(self.chunks[group], self.targets[group], self.sems.at[group])
        copy.start()
        self.started.append(copy)

    def finish(self):
        finish(self.started)


def dam_part_kernel(
    capacity,
    dam,
    free_hbm,
    dam_conn_hbm,
    dam_hbm,
    stiff_hbm,
    stiff_coef_hbm,
    mass_coef_hbm,
    back_hbm,
    order_ref,
    columns_ref,
    force_hbm,
    free_ref,
    dam_conn_ref,
    dam_ref,
    stiff_ref,
    stiff_coef_ref,
    mass_coef_ref,
    back_ref,
    force_ref,
    held0,
    held1,
    sems,
    force_sems,
):
    inward = transfer(
        [
            (dam_conn_hbm, dam_conn_ref),
            (dam_hbm, dam_ref),
            (stiff_hbm, stiff_ref),
            (free_hbm, free_ref),
            (stiff_coef_hbm, stiff_coef_ref),
            (mass_coef_hbm, mass_coef_ref),
        ],
        sems,
    )
    finish(inward)
    order_ref[...] = by_component(stiff_ref[...])
    dam_columns = dam_conn_ref[...].T
    free_columns = free_ref[...].T
    sender_of = free_columns // capacity
    free_columns = free_columns + (block_of(sender_of, dam) - sender_of) * capacity
    nodes = free_columns.shape[0]
    for e in range(free_columns.shape[1]):
        own = jnp.broadcast_to(free_columns[:, e : e + 1], (nodes, LANES))
        columns_ref[e * nodes : (e + 1) * nodes, :] = own.astype(jnp.int16)
    groups = force_sems.shape[0]
    held = (held0, held1)
    sender = Sender(force_ref, force_hbm, force_sems)

    def gather(group):
        select = select_rows(dam_columns, group * GROUP, dam_ref.shape[0])
        held[group % 2][...] = dot(select, dam_ref[...]).astype(BF16)

    def add(group):
        sender.start(group)
        select = select_spread(chunks_of(columns_ref, groups)[group][...], back_ref.shape[1])
        part = dot_first(sender.chunks[group][...], select)
        back_ref[...] = part if group == 0 else back_ref[...] + part

    coefs = (stiff_coef_ref, mass_coef_ref)
    sweep(groups, gather, forces_stage(held, order_ref, coefs, sender.chunks), add)
    finish(transfer([(back_ref, back_hbm)], sems))
    sender.finish()


def free_part_kernel(
    columns_ref,
    received_ref,
    order_ref,
    stiff_coef_hbm,
    mass_coef_hbm,
    start_hbm,
    force_hbm,
    back_hbm,
    stiff_coef_ref,
    mass_coef_ref,
    start_ref,
    total_ref,
    made,
    force_ref,
    back_ref,
    held0,
    held1,
    sems,
    force_sems,
):
    inward = transfer(
        [
            (stiff_coef_hbm, stiff_coef_ref),
            (mass_coef_hbm, mass_coef_ref),
            (start_hbm, start_ref),
        ],
        sems,
    )
    groups = force_sems.shape[0]
    made_chunks = chunks_of(made, groups)
    held = (held0, held1)
    sender = Sender(force_ref, force_hbm, force_sems)

    def gather(group):
        select = select_spread(chunks_of(columns_ref, groups)[group][...], received_ref.shape[0])
        held[group % 2][...] = dot(select, received_ref[...]).astype(BF16)
        if group == 0:
            finish(inward[:2])

    def add(group):
        sender.start(group)
        part = dot_first(
            sender.chunks[group][...],
            select_spread(chunks_of(columns_ref, groups)[group][...], received_ref.shape[0]),
        )
        total_ref[...] = part if group == 0 else total_ref[...] + part

    coefs = (stiff_coef_ref, mass_coef_ref)
    sweep(groups, gather, forces_stage(held, order_ref, coefs, sender.chunks), add)
    finish(inward[2:])
    slots = total_ref.shape[1]
    quarter = slots // 4
    outward = []
    for i in range(4):
        rows = slice(i * quarter, (i + 1) * quarter)
        back_ref[rows, :] = (start_ref[:, rows] + total_ref[:, rows]).T.astype(BF16)
        copy = pltpu.make_async_copy(back_ref.at[rows, :], back_hbm.at[rows, :], sems.at[i])
        copy.start()
        outward.append(copy)
    finish(outward)
    sender.finish()


def dam_update_kernel(
    dam_conn_hbm,
    free_force_hbm,
    dam_force_hbm,
    dam_hbm,
    step_hbm,
    next_hbm,
    dam_conn_ref,
    free_force,
    dam_force,
    total_ref,
    dam_ref,
    step_ref,
    next_ref,
    sems,
    free_sems,
    dam_sems,
):
    groups = free_sems.shape[0]
    inward = transfer([(dam_conn_hbm, dam_conn_ref), (dam_hbm, dam_ref), (step_hbm, step_ref)], sems)
    free_chunks, dam_chunks = chunks_of(free_force, groups), chunks_of(dam_force, groups)
    free_copies = transfer(list(zip(chunks_of(free_force_hbm, groups), free_chunks)), free_sems)
    dam_copies = transfer(list(zip(chunks_of(dam_force_hbm, groups), dam_chunks)), dam_sems)
    finish(inward)
    columns = dam_conn_ref[...].T
    for group in range(groups):
        finish([free_copies[group], dam_copies[group]])
        force = free_chunks[group][...].astype(F32) + dam_chunks[group][...].astype(F32)
        select = select_rows(columns, group * GROUP, dam_ref.shape[0])
        part = dot_first(force.astype(BF16), select)
        total_ref[...] = part if group == 0 else total_ref[...] + part
    step = as_column(step_ref[...])
    next_ref[...] = (dam_ref[...].astype(F32) - step * total_ref[...].T).astype(BF16)
    finish(transfer([(next_ref, next_hbm)], sems))


def exchange(rows, devices, capacity):
    width = rows.shape[1]
    shaped = rows.reshape(devices, capacity, width)
    arrived = lax.all_to_all(shaped, AXES, split_axis=0, concat_axis=0, tiled=True)
    return arrived.reshape(devices * capacity, width)


def kernel(body, name, ins, outs, scratch, flops=0, moved=0):
    hbm = pl.BlockSpec(memory_space=pltpu.HBM)
    vmem = pl.BlockSpec(memory_space=pltpu.VMEM)
    spaces = {"h": pltpu.HBM, "v": pltpu.VMEM}
    call = pl.pallas_call(
        body,
        name=name,
        in_specs=[hbm if letter == "h" else vmem for letter in ins],
        out_specs=[hbm if out[0] == "h" else vmem for out in outs],
        out_shape=[spaces[out[0]](*out[1:]) for out in outs],
        scratch_shapes=scratch,
        compiler_params=pltpu.CompilerParams(vmem_limit_bytes=VMEM_BYTES),
        cost_estimate=pl.CostEstimate(flops=flops, bytes_accessed=moved, transcendentals=0),
    )

    def run(*operands):
        return call(
            *[
                x if letter == "a" else pltpu.with_memory_space_constraint(x, spaces[letter])
                for letter, x in zip(ins, operands)
            ]
        )

    return run


def shards(
    history,
    routes,
    dam_field,
    conn_free,
    conn_dam,
    stiff_ref,
    stiff_coef,
    mass_coef,
    reg_step,
    dam_step,
):
    devices = lax.axis_size(AXES)
    row_count, width = history.shape
    capacity = 4 * row_count // devices
    slots = devices * capacity
    dam_count = dam_field.shape[0]
    elements, nodes = conn_free.shape
    all_pairs = elements * nodes
    pairs = GROUP * nodes
    groups = elements // GROUP

    I32 = jnp.int32
    vmem = pltpu.VMEM
    dma = pltpu.SemaphoreType.DMA
    conn = vmem((elements, nodes), I32)
    stiff = vmem(stiff_ref.shape, BF16)
    coefs = [pltpu.SMEM((elements,), F32)] * 2
    held = [vmem((pairs, width), BF16)] * 2
    forces_type = ((all_pairs, width), BF16)
    free_type = ((all_pairs, slots), BF16)
    back_type = ((width, slots), F32)
    stiff_type = (stiff_ref.shape, BF16)
    place_type = ((slots, row_count), BF16)
    slots_type = ((slots, width), BF16)
    rows_type = ((row_count, width), BF16)
    pulled_type = ((row_count, width), F32)
    column_type = ((row_count, 128), F32)
    dam_type = ((dam_count, width), BF16)
    product = 2 * all_pairs * slots * width

    pack = kernel(
        functools.partial(pack_kernel, capacity, lax.axis_size("dam")),
        "pack",
        "hhh",
        [("h", *slots_type), ("v", *place_type), ("v", *rows_type), ("v", *column_type)],
        [vmem((2, row_count), I32), vmem((1, row_count), F32), vmem(*slots_type), dma((3,))],
    )
    turn = kernel(
        turn_kernel,
        "turn",
        "vavvh",
        [("v", *rows_type), ("h", *slots_type)],
        [vmem(*slots_type), dma((1,))],
    )
    last = kernel(
        last_kernel,
        "last",
        "vavvh",
        [("h", *rows_type), ("h", *pulled_type)],
        [vmem(*rows_type), vmem(*pulled_type), dma((2,))],
    )
    dam_part = kernel(
        functools.partial(dam_part_kernel, capacity, lax.axis_size("dam")),
        "dam_part",
        "hhhhhh",
        [("h", *back_type), ("v", *stiff_type), ("v", (all_pairs, LANES), jnp.int16), ("h", *forces_type)],
        [conn, conn, vmem(*dam_type), stiff, *coefs, vmem(*back_type), vmem(*forces_type)]
        + [*held, dma((6,)), dma((groups,))],
        flops=3 * product,
        moved=4 * all_pairs * width,
    )
    free_part = kernel(
        free_part_kernel,
        "free_part",
        "vavhhh",
        [("h", *forces_type), ("h", *slots_type)],
        [*coefs, vmem(*back_type), vmem(*back_type)]
        + [vmem(*free_type), vmem(*forces_type), vmem(*slots_type), *held]
        + [dma((4,)), dma((groups,))],
        flops=3 * product,
        moved=4 * all_pairs * width,
    )
    dam_update = kernel(
        dam_update_kernel,
        "dam_update",
        "hhhhh",
        [("h", *dam_type)],
        [conn, vmem(*forces_type), vmem(*forces_type)]
        + [vmem((width, dam_count), F32), vmem(*dam_type), vmem((1, dam_count), F32)]
        + [vmem(*dam_type), dma((3,)), dma((groups,)), dma((groups,))],
        flops=product,
        moved=4 * all_pairs * width,
    )

    reg_row = reg_step.reshape(1, row_count)
    dam_row = dam_step.reshape(1, dam_count)
    outgoing, place, history, reg_column = pack(routes.T, history, reg_row)
    for round_index in range(ROUNDS):
        received = exchange(outgoing, devices, capacity)
        back_start, ordered, columns, dam_force = dam_part(
            conn_free, conn_dam, dam_field, stiff_ref, stiff_coef, mass_coef
        )
        free_force, back = free_part(
            columns, received, ordered, stiff_coef, mass_coef, back_start
        )
        returned = exchange(back, devices, capacity)
        (dam_field,) = dam_update(conn_dam, free_force, dam_force, dam_field, dam_row)
        if round_index < ROUNDS - 1:
            history, outgoing = turn(place, returned, history, reg_column, dam_field)
        else:
            history, pulled = last(place, returned, history, reg_column, dam_field)
    return (history, pulled, dam_field)


def solution(mesh):
    reg, dam = mesh.devices.shape
    split = Mesh(mesh.devices.reshape(reg // 2, 2, dam), ("reg_high", "reg_low", "dam"))
    axes = ("reg_high", "reg_low", "dam")
    rows = P(axes, None)
    flat = P(axes)
    in_specs = (rows, rows, rows, rows, rows, P(), flat, flat, flat, flat)
    return jax.shard_map(
        shards, mesh=split, in_specs=in_specs, out_specs=(rows, rows, rows), check_vma=False
    )
```

```python
import functools

import jax
import jax.numpy as jnp
from jax import lax
from jax.experimental import pallas as pl
from jax.experimental.pallas import tpu as pltpu
from jax.sharding import Mesh
from jax.sharding import PartitionSpec as P

ROUNDS = 2
AXES = ("reg_high", "dam", "reg_low")
GROUP = 16
LANES = 128
VMEM_BYTES = 28 * 1024 * 1024
BF16 = jnp.bfloat16
F32 = jnp.float32


def mask_to_bf16(mask):
    return jnp.where(mask, 1.0, 0.0).astype(BF16)


def dot(left, right):
    return jnp.dot(left, right, preferred_element_type=F32)


def dot_first(left, right):
    return lax.dot_general(left, right, (((0,), (0,)), ((), ())), preferred_element_type=F32)


def transfer(pairs, sems):
    copies = [pltpu.make_async_copy(a, b, sems.at[i]) for i, (a, b) in enumerate(pairs)]
    for copy in copies:
        copy.start()
    return copies


def finish(copies):
    for copy in copies:
        copy.wait()


def as_column(row):
    size = row.shape[1]
    down = lax.broadcasted_iota(jnp.int32, (size, size), 0)
    across = lax.broadcasted_iota(jnp.int32, (size, size), 1)
    return jnp.sum(jnp.where(down == across, row, jnp.zeros_like(row)), axis=1, keepdims=True)


def send_product(place_ref, rows, out_ref, out_hbm, sems):
    parts = sems.shape[0]
    size = out_ref.shape[0] // parts
    copies = []
    for i in range(parts):
        part = slice(i * size, (i + 1) * size)
        out_ref[part, :] = dot(place_ref[part, :], rows).astype(BF16)
        copies.append(pltpu.make_async_copy(out_ref.at[part, :], out_hbm.at[part, :], sems.at[i]))
        copies[-1].start()
    return copies


def block_of(device, dam):
    high = device // (2 * dam)
    rest = device - high * (2 * dam)
    low = rest // dam
    return (high * dam + rest - low * dam) * 2 + low


def pack_kernel(
    capacity,
    dam,
    routes_hbm,
    history_hbm,
    step_hbm,
    out_hbm,
    place_ref,
    history_ref,
    column_ref,
    routes_ref,
    step_ref,
    out_ref,
    sems,
    out_sems,
):
    inward = transfer(
        [(routes_hbm, routes_ref), (history_hbm, history_ref), (step_hbm, step_ref)], sems
    )
    slots, rows = place_ref.shape
    down = lax.broadcasted_iota(jnp.int32, (rows, rows), 0)
    across = lax.broadcasted_iota(jnp.int32, (rows, rows), 1)
    earlier = mask_to_bf16(down < across)
    devices = lax.broadcasted_iota(jnp.int32, (slots // capacity, rows), 0)
    numbers = lax.broadcasted_iota(jnp.int32, (slots, rows), 0)
    finish(inward[:1])
    own = [routes_ref[0:1, :], routes_ref[1:2, :]]
    named = [row == devices for row in own]
    before = dot(mask_to_bf16(named[0] | named[1]), earlier)
    hits = []
    for row, mask in zip(own, named):
        slot = jnp.sum(jnp.where(mask, before, 0.0), axis=0, keepdims=True).astype(jnp.int32)
        hits.append(block_of(row, dam) * capacity + slot == numbers)
    place = mask_to_bf16(hits[0] | hits[1])
    place_ref[...] = place
    finish(inward[1:2])
    history = history_ref[...]
    outward = send_product(place_ref, history, out_ref, out_hbm, out_sems)
    finish(inward[2:])
    column_ref[...] = jnp.broadcast_to(as_column(step_ref[...]), column_ref.shape)
    finish(outward)


def turn_kernel(
    place_ref, returned_ref, history_ref, column_ref, after_hbm, next_ref, out_hbm, out_ref, sems
):
    pulled = dot_first(place_ref[...], returned_ref[...])
    following = (history_ref[...].astype(F32) - column_ref[:, 0:1] * pulled).astype(BF16)
    next_ref[...] = following
    finish(send_product(place_ref, following, out_ref, out_hbm, sems))


def last_kernel(
    place_ref,
    returned_ref,
    history_ref,
    column_ref,
    after_hbm,
    next_hbm,
    pulled_hbm,
    next_ref,
    pulled_ref,
    sems,
):
    pulled = dot_first(place_ref[...], returned_ref[...])
    pulled_ref[...] = pulled
    outward = transfer([(pulled_ref, pulled_hbm)], sems)
    next_ref[...] = (history_ref[...].astype(F32) - column_ref[:, 0:1] * pulled).astype(BF16)
    finish(outward + transfer([(next_ref, next_hbm)], sems.at[1:2]))


def by_component(stiff):
    size = stiff.shape[0]
    nodes = size // 3
    down = lax.broadcasted_iota(jnp.int32, (size, size), 0)
    across = lax.broadcasted_iota(jnp.int32, (size, size), 1)
    part = (down >= nodes).astype(jnp.int32) + (down >= 2 * nodes).astype(jnp.int32)
    order = mask_to_bf16(across == 3 * (down - part * nodes) + part)
    half = dot(order, stiff).astype(BF16)
    return lax.dot_general(
        half, order, (((1,), (1,)), ((), ())), preferred_element_type=F32
    ).astype(BF16)


def select_rows(columns, first, width):
    nodes = columns.shape[0]
    lanes = lax.broadcasted_iota(jnp.int32, (nodes, width), 1).astype(jnp.int16)
    parts = []
    for e in range(first, first + GROUP):
        own = jnp.broadcast_to(columns[:, e : e + 1], (nodes, LANES)).astype(jnp.int16)
        own = jnp.concatenate([own] * (width // LANES), axis=1)
        parts.append(jnp.where(own == lanes, jnp.ones((), BF16), jnp.zeros((), BF16)))
    return jnp.concatenate(parts, axis=0)


def select_spread(spread, width):
    own = jnp.concatenate([spread] * (width // LANES), axis=1)
    lanes = lax.broadcasted_iota(jnp.int32, own.shape, 1).astype(jnp.int16)
    return jnp.where(own == lanes, jnp.ones((), BF16), jnp.zeros((), BF16))


def element_forces(u, stiff, stiff_coef_ref, mass_coef_ref, first):
    nodes = u.shape[0] // GROUP
    samples = u.shape[1] // 3
    lane = lax.broadcasted_iota(jnp.int32, (nodes, samples), 1).astype(jnp.int16)
    nothing = jnp.zeros((), BF16)

    def part(e, c):
        return u[e * nodes : (e + 1) * nodes, c * samples : (c + 1) * samples]

    blocks = []
    for pair in range(0, GROUP, 2):
        sides = [jnp.concatenate([part(e, c) for c in range(3)], axis=0) for e in (pair, pair + 1)]
        product = dot(stiff, jnp.concatenate(sides, axis=1))
        for side, e in enumerate((pair, pair + 1)):
            k = stiff_coef_ref[first + e]
            m = mass_coef_ref[first + e]
            row = []
            for c in range(3):
                own = product[c * nodes : (c + 1) * nodes, side * samples : (side + 1) * samples]
                w = part(e, c)
                before = jnp.where(lane == 0, nothing, pltpu.roll(w, 1, 1))
                after = jnp.where(lane == samples - 1, nothing, pltpu.roll(w, samples - 1, 1))
                accel = ((after - w) + (before - w)).astype(F32)
                row.append((k * own + m * accel).astype(BF16))
            blocks.append(jnp.concatenate(row, axis=1))
    return jnp.concatenate(blocks, axis=0)


def chunks_of(ref, groups):
    rows = ref.shape[0] // groups
    return [ref.at[g * rows : (g + 1) * rows, :] for g in range(groups)]


def sweep(groups, gather, forces, add):
    for turn in range(groups + 2):
        if turn >= 2:
            add(turn - 2)
        if 1 <= turn <= groups:
            forces(turn - 1)
        if turn < groups:
            gather(turn)


def forces_stage(held, stiff_ref, coefs, force_chunks):
    def stage(group):
        force_chunks[group][...] = element_forces(
            held[group % 2][...], stiff_ref[...], *coefs, group * GROUP
        )

    return stage


class Sender:
    def __init__(self, source, target, sems):
        self.chunks = chunks_of(source, sems.shape[0])
        self.targets = chunks_of(target, sems.shape[0])
        self.sems = sems
        self.started = []

    def start(self, group):
        copy = pltpu.make_async_copy(self.chunks[group], self.targets[group], self.sems.at[group])
        copy.start()
        self.started.append(copy)

    def finish(self):
        finish(self.started)


def dam_part_kernel(
    capacity,
    dam,
    free_hbm,
    dam_conn_hbm,
    dam_hbm,
    stiff_hbm,
    stiff_coef_hbm,
    mass_coef_hbm,
    back_hbm,
    order_ref,
    columns_ref,
    force_hbm,
    free_ref,
    dam_conn_ref,
    dam_ref,
    stiff_ref,
    stiff_coef_ref,
    mass_coef_ref,
    back_ref,
    force_ref,
    held0,
    held1,
    sems,
    force_sems,
):
    inward = transfer(
        [
            (dam_conn_hbm, dam_conn_ref),
            (dam_hbm, dam_ref),
            (stiff_hbm, stiff_ref),
            (free_hbm, free_ref),
            (stiff_coef_hbm, stiff_coef_ref),
            (mass_coef_hbm, mass_coef_ref),
        ],
        sems,
    )
    finish(inward)
    order_ref[...] = by_component(stiff_ref[...])
    dam_columns = dam_conn_ref[...].T
    free_columns = free_ref[...].T
    sender_of = free_columns // capacity
    free_columns = free_columns + (block_of(sender_of, dam) - sender_of) * capacity
    nodes = free_columns.shape[0]
    for e in range(free_columns.shape[1]):
        own = jnp.broadcast_to(free_columns[:, e : e + 1], (nodes, LANES))
        columns_ref[e * nodes : (e + 1) * nodes, :] = own.astype(jnp.int16)
    groups = force_sems.shape[0]
    held = (held0, held1)
    sender = Sender(force_ref, force_hbm, force_sems)

    def gather(group):
        select = select_rows(dam_columns, group * GROUP, dam_ref.shape[0])
        held[group % 2][...] = dot(select, dam_ref[...]).astype(BF16)

    def add(group):
        sender.start(group)
        select = select_spread(chunks_of(columns_ref, groups)[group][...], back_ref.shape[1])
        part = dot_first(sender.chunks[group][...], select)
        back_ref[...] = part if group == 0 else back_ref[...] + part

    coefs = (stiff_coef_ref, mass_coef_ref)
    sweep(groups, gather, forces_stage(held, order_ref, coefs, sender.chunks), add)
    finish(transfer([(back_ref, back_hbm)], sems))
    sender.finish()


def free_part_kernel(
    columns_ref,
    received_ref,
    order_ref,
    stiff_coef_hbm,
    mass_coef_hbm,
    start_hbm,
    force_hbm,
    back_hbm,
    stiff_coef_ref,
    mass_coef_ref,
    start_ref,
    total_ref,
    force_ref,
    back_ref,
    held0,
    held1,
    sems,
    force_sems,
):
    inward = transfer(
        [
            (stiff_coef_hbm, stiff_coef_ref),
            (mass_coef_hbm, mass_coef_ref),
            (start_hbm, start_ref),
        ],
        sems,
    )
    groups = force_sems.shape[0]
    held = (held0, held1)
    sender = Sender(force_ref, force_hbm, force_sems)

    def gather(group):
        select = select_spread(chunks_of(columns_ref, groups)[group][...], received_ref.shape[0])
        held[group % 2][...] = dot(select, received_ref[...]).astype(BF16)
        if group == 0:
            finish(inward[:2])

    def add(group):
        sender.start(group)
        part = dot_first(
            sender.chunks[group][...],
            select_spread(chunks_of(columns_ref, groups)[group][...], received_ref.shape[0]),
        )
        total_ref[...] = part if group == 0 else total_ref[...] + part

    coefs = (stiff_coef_ref, mass_coef_ref)
    sweep(groups, gather, forces_stage(held, order_ref, coefs, sender.chunks), add)
    finish(inward[2:])
    slots = total_ref.shape[1]
    quarter = slots // 4
    outward = []
    for i in range(4):
        rows = slice(i * quarter, (i + 1) * quarter)
        back_ref[rows, :] = (start_ref[:, rows] + total_ref[:, rows]).T.astype(BF16)
        copy = pltpu.make_async_copy(back_ref.at[rows, :], back_hbm.at[rows, :], sems.at[i])
        copy.start()
        outward.append(copy)
    finish(outward)
    sender.finish()


def dam_update_kernel(
    dam_conn_hbm,
    free_force_hbm,
    dam_force_hbm,
    dam_hbm,
    step_hbm,
    next_hbm,
    dam_conn_ref,
    free_force,
    dam_force,
    total_ref,
    dam_ref,
    step_ref,
    next_ref,
    sems,
    free_sems,
    dam_sems,
):
    groups = free_sems.shape[0]
    inward = transfer([(dam_conn_hbm, dam_conn_ref), (dam_hbm, dam_ref), (step_hbm, step_ref)], sems)
    free_chunks, dam_chunks = chunks_of(free_force, groups), chunks_of(dam_force, groups)
    free_copies = transfer(list(zip(chunks_of(free_force_hbm, groups), free_chunks)), free_sems)
    dam_copies = transfer(list(zip(chunks_of(dam_force_hbm, groups), dam_chunks)), dam_sems)
    finish(inward)
    columns = dam_conn_ref[...].T
    for group in range(groups):
        finish([free_copies[group], dam_copies[group]])
        force = free_chunks[group][...].astype(F32) + dam_chunks[group][...].astype(F32)
        select = select_rows(columns, group * GROUP, dam_ref.shape[0])
        part = dot_first(force.astype(BF16), select)
        total_ref[...] = part if group == 0 else total_ref[...] + part
    step = as_column(step_ref[...])
    next_ref[...] = (dam_ref[...].astype(F32) - step * total_ref[...].T).astype(BF16)
    finish(transfer([(next_ref, next_hbm)], sems))


def exchange(rows, devices, capacity):
    width = rows.shape[1]
    shaped = rows.reshape(devices, capacity, width)
    arrived = lax.all_to_all(shaped, AXES, split_axis=0, concat_axis=0, tiled=True)
    return arrived.reshape(devices * capacity, width)


def kernel(body, name, ins, outs, scratch, flops=0, moved=0):
    hbm = pl.BlockSpec(memory_space=pltpu.HBM)
    vmem = pl.BlockSpec(memory_space=pltpu.VMEM)
    spaces = {"h": pltpu.HBM, "v": pltpu.VMEM}
    call = pl.pallas_call(
        body,
        name=name,
        in_specs=[hbm if letter == "h" else vmem for letter in ins],
        out_specs=[hbm if out[0] == "h" else vmem for out in outs],
        out_shape=[spaces[out[0]](*out[1:]) for out in outs],
        scratch_shapes=scratch,
        compiler_params=pltpu.CompilerParams(vmem_limit_bytes=VMEM_BYTES),
        cost_estimate=pl.CostEstimate(flops=flops, bytes_accessed=moved, transcendentals=0),
    )

    def run(*operands):
        return call(
            *[
                x if letter == "a" else pltpu.with_memory_space_constraint(x, spaces[letter])
                for letter, x in zip(ins, operands)
            ]
        )

    return run


def shards(
    history,
    routes,
    dam_field,
    conn_free,
    conn_dam,
    stiff_ref,
    stiff_coef,
    mass_coef,
    reg_step,
    dam_step,
):
    devices = lax.axis_size(AXES)
    row_count, width = history.shape
    capacity = 4 * row_count // devices
    slots = devices * capacity
    dam_count = dam_field.shape[0]
    elements, nodes = conn_free.shape
    all_pairs = elements * nodes
    pairs = GROUP * nodes
    groups = elements // GROUP

    I32 = jnp.int32
    vmem = pltpu.VMEM
    dma = pltpu.SemaphoreType.DMA
    conn = vmem((elements, nodes), I32)
    stiff = vmem(stiff_ref.shape, BF16)
    coefs = [pltpu.SMEM((elements,), F32)] * 2
    held = [vmem((pairs, width), BF16)] * 2
    forces_type = ((all_pairs, width), BF16)
    back_type = ((width, slots), F32)
    stiff_type = (stiff_ref.shape, BF16)
    place_type = ((slots, row_count), BF16)
    slots_type = ((slots, width), BF16)
    rows_type = ((row_count, width), BF16)
    pulled_type = ((row_count, width), F32)
    column_type = ((row_count, 128), F32)
    dam_type = ((dam_count, width), BF16)
    product = 2 * all_pairs * slots * width

    pack = kernel(
        functools.partial(pack_kernel, capacity, lax.axis_size("dam")),
        "pack",
        "hhh",
        [("h", *slots_type), ("v", *place_type), ("v", *rows_type), ("v", *column_type)],
        [vmem((2, row_count), I32), vmem((1, row_count), F32), vmem(*slots_type), dma((3,)), dma((2,))],
    )
    turn = kernel(
        turn_kernel,
        "turn",
        "vavvh",
        [("v", *rows_type), ("h", *slots_type)],
        [vmem(*slots_type), dma((2,))],
    )
    last = kernel(
        last_kernel,
        "last",
        "vavvh",
        [("h", *rows_type), ("h", *pulled_type)],
        [vmem(*rows_type), vmem(*pulled_type), dma((2,))],
    )
    dam_part = kernel(
        functools.partial(dam_part_kernel, capacity, lax.axis_size("dam")),
        "dam_part",
        "hhhhhh",
        [("h", *back_type), ("v", *stiff_type), ("v", (all_pairs, LANES), jnp.int16), ("h", *forces_type)],
        [conn, conn, vmem(*dam_type), stiff, *coefs, vmem(*back_type), vmem(*forces_type)]
        + [*held, dma((6,)), dma((groups,))],
        flops=3 * product,
        moved=4 * all_pairs * width,
    )
    free_part = kernel(
        free_part_kernel,
        "free_part",
        "vavhhh",
        [("h", *forces_type), ("h", *slots_type)],
        [*coefs, vmem(*back_type), vmem(*back_type)]
        + [vmem(*forces_type), vmem(*slots_type), *held]
        + [dma((4,)), dma((groups,))],
        flops=3 * product,
        moved=4 * all_pairs * width,
    )
    dam_update = kernel(
        dam_update_kernel,
        "dam_update",
        "hhhhh",
        [("h", *dam_type)],
        [conn, vmem(*forces_type), vmem(*forces_type)]
        + [vmem((width, dam_count), F32), vmem(*dam_type), vmem((1, dam_count), F32)]
        + [vmem(*dam_type), dma((3,)), dma((groups,)), dma((groups,))],
        flops=product,
        moved=4 * all_pairs * width,
    )

    reg_row = reg_step.reshape(1, row_count)
    dam_row = dam_step.reshape(1, dam_count)
    outgoing, place, history, reg_column = pack(routes.T, history, reg_row)
    for round_index in range(ROUNDS):
        received = exchange(outgoing, devices, capacity)
        back_start, ordered, columns, dam_force = dam_part(
            conn_free, conn_dam, dam_field, stiff_ref, stiff_coef, mass_coef
        )
        free_force, back = free_part(
            columns, received, ordered, stiff_coef, mass_coef, back_start
        )
        returned = exchange(back, devices, capacity)
        (dam_field,) = dam_update(conn_dam, free_force, dam_force, dam_field, dam_row)
        if round_index < ROUNDS - 1:
            history, outgoing = turn(place, returned, history, reg_column, dam_field)
        else:
            history, pulled = last(place, returned, history, reg_column, dam_field)
    return (history, pulled, dam_field)


def solution(mesh):
    reg, dam = mesh.devices.shape
    split = Mesh(mesh.devices.reshape(reg // 2, 2, dam), ("reg_high", "reg_low", "dam"))
    axes = ("reg_high", "reg_low", "dam")
    rows = P(axes, None)
    flat = P(axes)
    in_specs = (rows, rows, rows, rows, rows, P(), flat, flat, flat, flat)
    return jax.shard_map(
        shards, mesh=split, in_specs=in_specs, out_specs=(rows, rows, rows), check_vma=False
    )
```
